512 devices in a mesh: prow: 32 (over x, z), pcol: 16 (over y, core).
Axes of the slice: x: 4, y: 8, z: 8, core: 2. Of those that a mesh axis runs over, the one named last changes fastest.
Arguments:
- sym_matrix: float32 [14336, 14336], P('prow', 'pcol'), may hold values from -4 to 4, as said below
- panel: float32 [14336, 128], P('prow', 'pcol'), may hold values from -0.06681531 to 0.06681531, as said below
Outputs:
- trailing: float32 [14336, 14336], P('prow', 'pcol')
- band_block: float32 [128, 128], replicated
The draws below stay inside these ranges and needn't reach their ends.
Inputs may be any that keep to these rules, and one draw needn't show every extreme that they name: `sym_matrix`: exactly symmetric. `panel`: of full column rank.
All inputs are finite; a program needn't handle non-finite values.
Results may differ from the reference program's by a relative error of at most 0.0001.
Values sent between devices are 32-bit elements; how exact they have to be, the bound alone decides.
No kernel may reach another device: no remote copies, remote signals or barrier semaphores. Data moves between devices by JAX's collectives and lax.ppermute only.
A program may use at most 64 MiB of HBM per device.

```python
import jax
import jax.numpy as jnp
from jax import lax

ORDER = 14336
NB = 128


def draw_sym_matrix(key, part):
    key = jax.random.fold_in(key, 11)
    base_draw = jnp.clip(jax.random.normal(key, (ORDER, ORDER), jnp.float32), -4.0, 4.0) * 0.7071
    return (base_draw + base_draw.T) * 0.7071


def draw_panel(key, part):
    key = jax.random.fold_in(key, 23)
    noise_key = jax.random.fold_in(key, 0)
    position = jnp.arange(ORDER, dtype=jnp.float32)[:, None] / ORDER
    noise_part = jnp.clip(jax.random.normal(noise_key, (ORDER, NB), jnp.float32), -4.0, 4.0)
    values = noise_part * jnp.sqrt(1.0 + 2.0 * position)
    return values * ORDER ** (-0.5)


def setup_inputs(seed: int = 0) -> dict:
    key_list = jax.random.split(jax.random.key(seed), 3)
    return {
        "sym_matrix": draw_sym_matrix(jax.random.fold_in(key_list[2], 71), 0),
        "panel": draw_panel(jax.random.fold_in(key_list[2], 71), 0),
    }


PRECISE = lax.Precision.HIGHEST
LU_STEP = 16

def matmul(left_operand, right_operand):
    return jnp.dot(left_operand, right_operand, precision=PRECISE, preferred_element_type=jnp.float32)

def cholesky_lower(gram_matrix):
    size_small = gram_matrix.shape[0]
    positions = jnp.arange(size_small, dtype=jnp.int32)

    def step(column_at, state):
        work, lower = state
        pivot = jnp.sqrt(work[column_at, column_at])
        column = jnp.where(positions >= column_at, work[:, column_at] / pivot, 0.0)
        trail = jnp.where(positions > column_at, column, 0.0)
        work = work - trail[:, None] * trail[None, :]
        lower = jnp.where((positions == column_at)[None, :], column[:, None], lower)
        return (work, lower)
    return lax.fori_loop(0, size_small, step, (gram_matrix, jnp.zeros_like(gram_matrix)))[1]

def solve_upper(upper, right_hand):
    size_small = upper.shape[0]
    positions = jnp.arange(size_small, dtype=jnp.int32)

    def step(count, solved):
        row_at = size_small - 1 - count
        row = jnp.where(positions > row_at, upper[row_at], 0.0)
        value = (right_hand[row_at] - matmul(row, solved)) / upper[row_at, row_at]
        return solved.at[row_at].set(value)
    return lax.fori_loop(0, size_small, step, jnp.zeros_like(right_hand))

def solve_unit_lower(lower, right_hand):
    size_small = lower.shape[0]
    positions = jnp.arange(size_small, dtype=jnp.int32)

    def step(row_at, solved):
        row = jnp.where(positions < row_at, lower[row_at], 0.0)
        value = right_hand[row_at] - matmul(row, solved)
        return solved.at[row_at].set(value)
    return lax.fori_loop(0, size_small, step, jnp.zeros_like(right_hand))

def eliminate_tall(tall):
    row_pos = jnp.arange(tall.shape[0], dtype=jnp.int32)
    col_pos = jnp.arange(tall.shape[1], dtype=jnp.int32)

    def eliminate(column_at, packed):
        pivot_value = packed[column_at, column_at]
        column = jnp.where(row_pos > column_at, packed[:, column_at] / pivot_value, 0.0)
        pivot_row = jnp.where(col_pos > column_at, packed[column_at, :], 0.0)
        packed = packed - column[:, None] * pivot_row[None, :]
        below = (col_pos[None, :] == column_at) & (row_pos[:, None] > column_at)
        return jnp.where(below, column[:, None], packed)
    return lax.fori_loop(0, tall.shape[1], eliminate, tall)

def factor_lower_upper(square):
    order_small = square.shape[0]
    width = min(LU_STEP, order_small)
    packed = square
    for start in range(0, order_small, width):
        finish = start + width
        tall = eliminate_tall(packed[start:, start:finish])
        packed = packed.at[start:, start:finish].set(tall)
        if finish < order_small:
            diag_part = tall[:width]
            small_pos = jnp.arange(width, dtype=jnp.int32)
            unit_lower = jnp.where(small_pos[:, None] > small_pos[None, :], diag_part, 0.0) + jnp.eye(width, dtype=square.dtype)
            right_rows = solve_unit_lower(unit_lower, packed[start:finish, finish:])
            packed = packed.at[start:finish, finish:].set(right_rows)
            packed = packed.at[finish:, finish:].add(-matmul(tall[width:], right_rows))
    positions = jnp.arange(order_small, dtype=jnp.int32)
    identity = jnp.eye(order_small, dtype=square.dtype)
    lower_l = jnp.where(positions[:, None] > positions[None, :], packed, 0.0) + identity
    upper_u = jnp.where(positions[:, None] <= positions[None, :], packed, 0.0)
    return (lower_l, upper_u)

def factor_panel(gram_matrix, top_rows):
    order_small = gram_matrix.shape[0]
    identity = jnp.eye(order_small, dtype=gram_matrix.dtype)
    upper_r = -cholesky_lower(gram_matrix).T
    inverse_r = solve_upper(upper_r, identity)
    lower_l, upper_u = factor_lower_upper(identity - matmul(top_rows, inverse_r))
    inverse_u = solve_upper(upper_u, identity)
    combine = matmul(inverse_r, inverse_u)
    tfactor = solve_unit_lower(lower_l, upper_u.T).T
    return (upper_r, lower_l, combine, tfactor)

def reference(sym_matrix, panel):
    gram_matrix = matmul(panel.T, panel)
    upper_r, lower_l, combine, tfactor = factor_panel(gram_matrix, panel[:NB])
    vectors = jnp.concatenate([lower_l, -matmul(panel[NB:], combine)], 0)
    product = matmul(sym_matrix, vectors)
    curvature = matmul(vectors.T, product)
    middle = matmul(tfactor.T, matmul(curvature, tfactor))
    update = matmul(product, tfactor) - 0.5 * matmul(vectors, middle)
    left_factor = jnp.concatenate([vectors, update], 1)
    right_factor = jnp.concatenate([update, vectors], 1)
    trailing = sym_matrix - matmul(left_factor, right_factor.T)
    return (trailing, upper_r)
```

```python
import jax
import jax.numpy as jnp
from jax import lax
from jax.experimental import pallas as pl
from jax.experimental.pallas import tpu as pltpu
from jax.sharding import PartitionSpec as P

PRECISE = lax.Precision.HIGHEST
VMEM_BYTES = 48 * 2**20
NB = 128
SUB = 8


def mm(left, right, contract=((1,), (0,))):
    return lax.dot_general(
        left, right, (contract, ((), ())), precision=PRECISE, preferred_element_type=jnp.float32
    )


def lane_ceil(count):
    return -(-count // NB) * NB


NT = ((1,), (1,))
TN = ((0,), (0,))


def first_rows_zeroed(block, is_first):
    lanes = lax.broadcasted_iota(jnp.int32, block.shape, 1)
    return jnp.where(is_first & (lanes < NB), 0.0, block)


def product_kernel(panels, matrix, sent):
    cols = matrix.shape[1]
    is_first = lax.axis_index("prow") == 0
    keep = jnp.where(is_first, 1.0, 0.0)
    own = pl.ds(pl.multiple_of(lax.axis_index("pcol") * SUB, SUB), SUB)
    rows_t = panels[:, cols:]
    part = mm(first_rows_zeroed(rows_t, is_first), matrix[...])
    gram = mm(panels[own, cols:], rows_t, NT)
    top = panels[own, cols : cols + NB] * keep
    half = NB // SUB
    for dest in range(half):
        sent[dest, :, :cols] = part[dest * SUB : (dest + 1) * SUB]
        sent[dest + half, :, :cols] = matrix[dest * SUB : (dest + 1) * SUB, :] * keep
    for dest in range(2 * half):
        sent[dest, :, cols : cols + NB] = gram
        sent[dest, :, cols + NB :] = top


def reduce_kernel(got, panels, sent):
    cols = panels.shape[1] - panels.shape[1] // 3
    is_first = lax.axis_index("pcol") == 0
    total = jnp.sum(got[...], axis=0)
    small = mm(total[:, :cols], first_rows_zeroed(panels[:, :cols], is_first), NT)
    corner = total[:, :NB] * jnp.where(is_first, 1.0, 0.0)
    for dest in range(sent.shape[0]):
        sent[dest, :, : cols + 2 * NB] = total
        sent[dest, :, cols + 2 * NB : cols + 3 * NB] = small
        sent[dest, :, cols + 3 * NB :] = corner


def spread_kernel(got, sent, gram, top_t):
    parts = got.shape[0]
    cols = got.shape[2] - 4 * NB
    rows = cols // 2
    at = lane_ceil(cols + rows)
    own = got[lax.axis_index("pcol"), :, :cols]
    corner = jnp.sum(got[:, :, cols + 2 * NB :], axis=0)
    for part in range(parts):
        gram[part * SUB : (part + 1) * SUB, :] = got[part, :, cols : cols + NB]
        top_t[part * SUB : (part + 1) * SUB, :] = got[part, :, cols + NB : cols + 2 * NB]
        whole = got[part, :, :cols]
        for half in range(2):
            dest = 2 * part + half
            sent[dest, :, :cols] = own
            sent[dest, :, cols : cols + rows] = whole[:, half * rows : (half + 1) * rows]
            sent[dest, :, cols + rows : at] = jnp.zeros((SUB, at - cols - rows), jnp.float32)
            sent[dest, :, at:] = corner


def factor_kernel(gram, top_t, band, inv_s, lower, tfac, work, inv_c, rest, inv_l, upper):
    rows = lax.broadcasted_iota(jnp.int32, (NB, NB), 0)
    lanes = lax.broadcasted_iota(jnp.int32, (NB, NB), 1)
    lane = lax.broadcasted_iota(jnp.int32, (1, NB), 1)
    eye = jnp.where(rows == lanes, 1.0, 0.0)
    work[...] = gram[...]
    rest[...] = -top_t[...].T
    inv_c[...] = eye
    inv_l[...] = eye
    inv_s[...] = eye
    scales = jnp.zeros((1, NB), jnp.float32)
    for k in range(NB):
        lo = (k // SUB) * SUB
        hi = lo + SUB
        below = rows[lo:, :1] > k
        inv = lax.rsqrt(work[k : k + 1, k : k + 1])
        c_row = jnp.where(lane >= k, work[k : k + 1, :] * inv, 0.0)
        band[k : k + 1, :] = -c_row
        c_col = jnp.where(below, work[lo:, k : k + 1] * inv, 0.0)
        x_row = inv_c[k : k + 1, :] * inv
        s_row = jnp.where(lane >= k, rest[k : k + 1, :] - c_row, 0.0)
        scale = 1.0 / (rest[k : k + 1, k : k + 1] - c_row[:, k : k + 1])
        l_col = jnp.where(below, rest[lo:, k : k + 1] * scale, 0.0)
        l_row = inv_l[k : k + 1, :]
        right = jnp.where(lane > k, s_row, 0.0)
        upper[k : k + 1, :] = s_row
        scales = jnp.where(lane == k, scale, scales)
        work[lo:, :] = work[lo:, :] - c_col * c_row
        inv_c[lo:, :] = jnp.where(rows[lo:] == k, x_row, inv_c[lo:, :] - c_col * x_row)
        rest[lo:, :] = rest[lo:, :] - l_col * right
        inv_l[lo:, :] = inv_l[lo:, :] - l_col * l_row
        s_col = inv_s[:hi, k : k + 1] * scale
        inv_s[:hi, :] = jnp.where(lanes[:hi] == k, s_col, inv_s[:hi, :] - s_col * right)
    lower[...] = jnp.where(rows > lanes, rest[...] * scales, eye)
    tfac[...] = -mm(upper[...], mm(inv_l[...], inv_c[...]), NT)


def update_kernel(panels, got, matrix, inv_s, lower, tfac, out):
    rows, cols = matrix.shape
    combine = -inv_s[...]
    low = lower[...]
    t = tfac[...]
    mix = jnp.concatenate([combine, low], 0)
    moved = got[:, : cols + rows]
    corner = got[:, lane_ceil(cols + rows) :]
    prod_t = mm(mix, moved, TN)
    curv = mm(mm(mix, corner, TN), mix)
    mid = mm(t, mm(curv, t), TN)
    is_row, is_col = lax.axis_index("prow") == 0, lax.axis_index("pcol") == 0
    vec_cols = mm(combine, first_rows_zeroed(panels[:, :cols], is_col), TN)
    vec_rows = mm(combine, first_rows_zeroed(panels[:, cols:], is_row), TN)
    low_t = low.T
    vec_cols = jnp.concatenate(
        [vec_cols[:, :NB] + low_t * jnp.where(is_col, 1.0, 0.0), vec_cols[:, NB:]], 1
    )
    vec_rows = jnp.concatenate(
        [vec_rows[:, :NB] + low_t * jnp.where(is_row, 1.0, 0.0), vec_rows[:, NB:]], 1
    )
    upd_t = mm(t, prod_t, TN)
    upd_cols = upd_t[:, :cols] - 0.5 * mm(mid, vec_cols, TN)
    upd_rows = upd_t[:, cols:] - 0.5 * mm(mid, vec_rows, TN)
    left = jnp.concatenate([vec_rows, upd_rows], 0)
    right = jnp.concatenate([upd_cols, vec_cols], 0)
    out[...] = matrix[...] - mm(left, right, TN)


def call(kernel, shapes, *args, scratch=(), cost=None):
    outs = [jax.ShapeDtypeStruct(s, jnp.float32) for s in shapes]
    return pl.pallas_call(
        kernel,
        out_shape=outs,
        scratch_shapes=[pltpu.VMEM(s, jnp.float32) for s in scratch],
        compiler_params=pltpu.CompilerParams(vmem_limit_bytes=VMEM_BYTES),
        cost_estimate=cost,
    )(*args)


def exchange(blocks, axis):
    return lax.all_to_all(blocks, axis, 0, 0)


def local(matrix, panel):
    rows, cols = matrix.shape
    n_row, n_col = lax.axis_size("prow"), lax.axis_size("pcol")
    block_t = panel.T
    column = exchange(jnp.broadcast_to(block_t[None], (n_row, SUB, rows)), "prow")
    column = column.reshape(n_col, 2, SUB, rows).transpose(0, 2, 1, 3).reshape(n_col, SUB, cols)
    own = jnp.broadcast_to(block_t[None], (n_col, SUB, rows))
    panels = exchange(jnp.concatenate([column, own], 2), "pcol").reshape(NB, cols + rows)
    (sent,) = call(product_kernel, [(n_row, SUB, cols + 2 * NB)], panels, matrix)
    (sent,) = call(reduce_kernel, [(n_col, SUB, cols + 4 * NB)], exchange(sent, "prow"), panels)
    wide = lane_ceil(cols + rows) + 2 * NB
    sent, gram, top_t = call(
        spread_kernel,
        [(n_row, SUB, wide), (NB, NB), (NB, NB)],
        exchange(sent, "pcol"),
    )
    got = exchange(sent, "prow").reshape(2 * NB, wide)
    small = (NB, NB)
    band, inv_s, lower, tfac = call(
        factor_kernel,
        [small] * 4,
        gram,
        top_t,
        scratch=[small] * 5,
        cost=pl.CostEstimate(flops=2 * 10**10, bytes_accessed=2**20, transcendentals=0),
    )
    (trailing,) = call(update_kernel, [(rows, cols)], panels, got, matrix, inv_s, lower, tfac)
    return (trailing, band)


def solution(mesh):
    specs = (P("prow", "pcol"), P("prow", "pcol"))
    return jax.shard_map(
        local, mesh=mesh, in_specs=specs, out_specs=(P("prow", "pcol"), P()), check_vma=False
    )
```

```python
import jax
import jax.numpy as jnp
from jax import lax
from jax.experimental import pallas as pl
from jax.experimental.pallas import tpu as pltpu
from jax.sharding import PartitionSpec as P

PRECISE = lax.Precision.HIGHEST
VMEM_BYTES = 48 * 2**20
NB = 128
SUB = 8
HALF = SUB // 2


def mm(left, right, contract=((1,), (0,))):
    return lax.dot_general(
        left, right, (contract, ((), ())), precision=PRECISE, preferred_element_type=jnp.float32
    )


def lane_ceil(count):
    return -(-count // NB) * NB


NT = ((1,), (1,))
TN = ((0,), (0,))


def first_rows_zeroed(block, is_first):
    lanes = lax.broadcasted_iota(jnp.int32, block.shape, 1)
    return jnp.where(is_first & (lanes < NB), 0.0, block)


def gram_kernel(rows_t, sent):
    own = pl.ds(pl.multiple_of(lax.axis_index("pcol") * SUB, SUB), SUB)
    block = rows_t[own, :]
    gram = mm(block, rows_t[...], NT)
    for dest in range(sent.shape[0]):
        sent[dest, :, :NB] = gram
        sent[dest, :, NB:] = block


def sort_kernel(got, small, blocks):
    rows = got.shape[2] - NB
    gram = jnp.sum(got[:, :, :NB], axis=0)
    for dest in range(small.shape[0]):
        small[dest, :, :NB] = gram
        small[dest, :, NB:] = got[0, :, NB : 2 * NB]
        blocks[dest, :, :rows] = got[2 * dest, :, NB:]
        blocks[dest, :, rows:] = got[2 * dest + 1, :, NB:]


def vectors(panel_t, combine, low, is_first):
    vec = mm(combine, first_rows_zeroed(panel_t, is_first), TN)
    head = vec[:, :NB] + low.T * jnp.where(is_first, 1.0, 0.0)
    return jnp.concatenate([head, vec[:, NB:]], 1)


def product_kernel(rows_t, matrix, inv_s, lower, vec_rows, sent):
    vec = vectors(rows_t[...], -inv_s[...], lower[...], lax.axis_index("prow") == 0)
    vec_rows[...] = vec
    part = mm(vec, matrix[...])
    for dest in range(sent.shape[0]):
        sent[dest] = part[dest * HALF : (dest + 1) * HALF]


def reduce_kernel(got, cols_t, inv_s, lower, vec_cols, sent):
    cols = cols_t.shape[1]
    vec = vectors(cols_t[...], -inv_s[...], lower[...], lax.axis_index("pcol") == 0)
    vec_cols[...] = vec
    total = jnp.sum(got[...], axis=0)
    small = mm(total, vec, NT)
    for dest in range(sent.shape[0]):
        sent[dest, :, :cols] = total
        sent[dest, :, cols:] = small


def spread_kernel(got, sent):
    cols = got.shape[2] - NB
    rows = cols // 2
    at = lane_ceil(cols + rows)
    own = got[lax.axis_index("pcol"), :, :cols]
    small = jnp.sum(got[:, :, cols:], axis=0)
    for part in range(got.shape[0]):
        whole = got[part, :, :cols]
        for half in range(2):
            dest = 2 * part + half
            sent[dest, :, :cols] = own
            sent[dest, :, cols : cols + rows] = whole[:, half * rows : (half + 1) * rows]
            sent[dest, :, cols + rows : at] = jnp.zeros((HALF, at - cols - rows), jnp.float32)
            sent[dest, :, at:] = small


def factor_kernel(got, band, inv_s, lower, tfac, work, inv_c, rest, inv_l, upper):
    rows = lax.broadcasted_iota(jnp.int32, (NB, NB), 0)
    lanes = lax.broadcasted_iota(jnp.int32, (NB, NB), 1)
    lane = lax.broadcasted_iota(jnp.int32, (1, NB), 1)
    eye = jnp.where(rows == lanes, 1.0, 0.0)
    for part in range(got.shape[0]):
        work[part * SUB : (part + 1) * SUB, :] = got[part, :, :NB]
        rest[part * SUB : (part + 1) * SUB, :] = -got[part, :, NB:]
    rest[...] = rest[...].T
    inv_c[...] = eye
    inv_l[...] = eye
    inv_s[...] = eye
    scales = jnp.zeros((1, NB), jnp.float32)
    for k in range(NB):
        lo = (k // SUB) * SUB
        hi = lo + SUB
        below = rows[lo:, :1] > k
        inv = lax.rsqrt(work[k : k + 1, k : k + 1])
        c_row = jnp.where(lane >= k, work[k : k + 1, :] * inv, 0.0)
        band[k : k + 1, :] = -c_row
        c_col = jnp.where(below, work[lo:, k : k + 1] * inv, 0.0)
        x_row = inv_c[k : k + 1, :] * inv
        s_row = jnp.where(lane >= k, rest[k : k + 1, :] - c_row, 0.0)
        scale = 1.0 / (rest[k : k + 1, k : k + 1] - c_row[:, k : k + 1])
        l_col = jnp.where(below, rest[lo:, k : k + 1] * scale, 0.0)
        l_row = inv_l[k : k + 1, :]
        right = jnp.where(lane > k, s_row, 0.0)
        upper[k : k + 1, :] = s_row
        scales = jnp.where(lane == k, scale, scales)
        work[lo:, :] = work[lo:, :] - c_col * c_row
        inv_c[lo:, :] = jnp.where(rows[lo:] == k, x_row, inv_c[lo:, :] - c_col * x_row)
        rest[lo:, :] = rest[lo:, :] - l_col * right
        inv_l[lo:, :] = inv_l[lo:, :] - l_col * l_row
        s_col = inv_s[:hi, k : k + 1] * scale
        inv_s[:hi, :] = jnp.where(lanes[:hi] == k, s_col, inv_s[:hi, :] - s_col * right)
    lower[...] = jnp.where(rows > lanes, rest[...] * scales, eye)
    tfac[...] = -mm(upper[...], mm(inv_l[...], inv_c[...]), NT)


def update_kernel(vec_rows, vec_cols, got, matrix, tfac, out, moved):
    rows, cols = matrix.shape
    at = lane_ceil(cols + rows)
    for part in range(got.shape[0]):
        moved[part * HALF : (part + 1) * HALF, :] = got[part]
    t = tfac[...]
    mid = mm(t, mm(moved[:, at:], t), TN)
    upd_cols = mm(t, moved[:, :cols], TN) - 0.5 * mm(mid, vec_cols[...])
    upd_rows = mm(t, moved[:, cols : cols + rows], TN) - 0.5 * mm(mid, vec_rows[...])
    left = jnp.concatenate([vec_rows[...], upd_rows], 0)
    right = jnp.concatenate([upd_cols, vec_cols[...]], 0)
    out[...] = matrix[...] - mm(left, right, TN)


def call(kernel, shapes, *args, scratch=(), cost=None):
    outs = [jax.ShapeDtypeStruct(s, jnp.float32) for s in shapes]
    return pl.pallas_call(
        kernel,
        out_shape=outs,
        scratch_shapes=[pltpu.VMEM(s, jnp.float32) for s in scratch],
        compiler_params=pltpu.CompilerParams(vmem_limit_bytes=VMEM_BYTES),
        cost_estimate=cost,
    )(*args)


def exchange(blocks, axis):
    return lax.all_to_all(blocks, axis, 0, 0)


def local(matrix, panel):
    rows, cols = matrix.shape
    n_row, n_col = lax.axis_size("prow"), lax.axis_size("pcol")
    block_t = jnp.broadcast_to(panel.T[None], (n_col, SUB, rows))
    rows_t = exchange(block_t, "pcol").reshape(NB, rows)
    (sent,) = call(gram_kernel, [(n_row, SUB, NB + rows)], rows_t)
    small, blocks = call(
        sort_kernel, [(n_col, SUB, 2 * NB), (n_col, SUB, cols)], exchange(sent, "prow")
    )
    band, inv_s, lower, tfac = call(
        factor_kernel,
        [(NB, NB)] * 4,
        exchange(small, "pcol"),
        scratch=[(NB, NB)] * 5,
        cost=pl.CostEstimate(flops=2 * 10**10, bytes_accessed=2**20, transcendentals=0),
    )
    cols_t = exchange(blocks, "pcol").reshape(NB, cols)
    vec_rows, sent = call(
        product_kernel, [(NB, rows), (n_row, HALF, cols)], rows_t, matrix, inv_s, lower
    )
    vec_cols, sent = call(
        reduce_kernel,
        [(NB, cols), (n_col, HALF, cols + NB)],
        exchange(sent, "prow"),
        cols_t,
        inv_s,
        lower,
    )
    wide = lane_ceil(cols + rows) + NB
    (sent,) = call(spread_kernel, [(n_row, HALF, wide)], exchange(sent, "pcol"))
    (trailing,) = call(
        update_kernel,
        [(rows, cols)],
        vec_rows,
        vec_cols,
        exchange(sent, "prow"),
        matrix,
        tfac,
        scratch=[(NB, wide)],
    )
    return (trailing, band)


def solution(mesh):
    specs = (P("prow", "pcol"), P("prow", "pcol"))
    return jax.shard_map(
        local, mesh=mesh, in_specs=specs, out_specs=(P("prow", "pcol"), P()), check_vma=False
    )
```

```python
import jax
import jax.numpy as jnp
from jax import lax
from jax.experimental import pallas as pl
from jax.experimental.pallas import tpu as pltpu
from jax.sharding import Mesh
from jax.sharding import PartitionSpec as P

PRECISE = lax.Precision.HIGHEST
VMEM_BYTES = 48 * 2**20
NB = 128
SUB = 8
PCOL = ("y", "core")


def pcol_index():
    return lax.axis_index("y") * lax.axis_size("core") + lax.axis_index("core")


def mm(left, right, contract=((1,), (0,))):
    return lax.dot_general(
        left, right, (contract, ((), ())), precision=PRECISE, preferred_element_type=jnp.float32
    )


def lane_ceil(count):
    return -(-count // NB) * NB


NT = ((1,), (1,))
TN = ((0,), (0,))


def first_rows_zeroed(block, is_first):
    lanes = lax.broadcasted_iota(jnp.int32, block.shape, 1)
    return jnp.where(is_first & (lanes < NB), 0.0, block)


def gram_kernel(rows_t, sent):
    own = pl.ds(pl.multiple_of(pcol_index() * SUB, SUB), SUB)
    block = rows_t[own, :]
    gram = mm(block, rows_t[...], NT)
    for dest in range(sent.shape[0]):
        sent[dest, :, :NB] = gram
        sent[dest, :, NB:] = block


def sort_kernel(got, small, blocks):
    rows = got.shape[2] - NB
    gram = jnp.sum(got[:, :, :NB], axis=0)
    for dest in range(small.shape[0]):
        small[dest, :, :NB] = gram
        small[dest, :, NB:] = got[0, :, NB : 2 * NB]
        blocks[dest, :, :rows] = got[2 * dest, :, NB:]
        blocks[dest, :, rows:] = got[2 * dest + 1, :, NB:]


def vectors(panel_t, combine, low, is_first):
    vec = mm(combine, first_rows_zeroed(panel_t, is_first), TN)
    head = vec[:, :NB] + low.T * jnp.where(is_first, 1.0, 0.0)
    return jnp.concatenate([head, vec[:, NB:]], 1)


def product_kernel(rows_t, cols_t, matrix, inv_s, lower, vec_rows, vec_cols, sent):
    combine, low = -inv_s[...], lower[...]
    vec_rows[...] = vectors(rows_t[...], combine, low, lax.axis_index("prow") == 0)
    vec = vectors(cols_t[...], combine, low, pcol_index() == 0)
    vec_cols[...] = vec
    part = mm(vec, matrix[...], NT)
    for dest in range(sent.shape[0]):
        sent[dest] = part[dest * SUB : (dest + 1) * SUB]


def reduce_kernel(got, vec_rows, sent):
    total = jnp.sum(got[...], axis=0)
    small = mm(total, vec_rows[...], NT)
    for dest in range(sent.shape[0]):
        sent[dest, :, :NB] = small
        sent[dest, :, NB:] = total


def spread_kernel(got, sent):
    rows = got.shape[2] - NB
    cols = 2 * rows
    at = lane_ceil(cols + rows)
    core = lax.axis_index("core")
    own = got[lax.axis_index("prow"), :, NB:]
    small = jnp.sum(got[:, :, :NB], axis=0)
    for dest in range(sent.shape[0]):
        here = 4 * dest + 2 * core
        there = 4 * dest + 2 * (1 - core)
        sent[dest, :, :rows] = got[there, :, NB:]
        sent[dest, :, rows:cols] = got[there + 1, :, NB:]
        sent[dest, :, cols : cols + rows] = own
        sent[dest, :, cols + rows : at] = jnp.zeros((SUB, at - cols - rows), jnp.float32)
        sent[dest, :, at : at + NB] = small
        sent[dest, :, at + NB : at + NB + rows] = got[here, :, NB:]
        sent[dest, :, at + NB + rows :] = got[here + 1, :, NB:]


def factor_kernel(got, band, inv_s, lower, tfac, work, inv_c, rest, inv_l, upper):
    rows = lax.broadcasted_iota(jnp.int32, (NB, NB), 0)
    lanes = lax.broadcasted_iota(jnp.int32, (NB, NB), 1)
    lane = lax.broadcasted_iota(jnp.int32, (1, NB), 1)
    eye = jnp.where(rows == lanes, 1.0, 0.0)
    for part in range(got.shape[0]):
        work[part * SUB : (part + 1) * SUB, :] = got[part, :, :NB]
        rest[part * SUB : (part + 1) * SUB, :] = -got[part, :, NB:]
    rest[...] = rest[...].T
    inv_c[...] = eye
    inv_l[...] = eye
    inv_s[...] = eye
    scales = jnp.zeros((1, NB), jnp.float32)
    for k in range(NB):
        lo = (k // SUB) * SUB
        hi = lo + SUB
        below = rows[lo:, :1] > k
        inv = lax.rsqrt(work[k : k + 1, k : k + 1])
        c_row = jnp.where(lane >= k, work[k : k + 1, :] * inv, 0.0)
        band[k : k + 1, :] = -c_row
        c_col = jnp.where(below, work[lo:, k : k + 1] * inv, 0.0)
        x_row = inv_c[k : k + 1, :] * inv
        s_row = jnp.where(lane >= k, rest[k : k + 1, :] - c_row, 0.0)
        scale = 1.0 / (rest[k : k + 1, k : k + 1] - c_row[:, k : k + 1])
        l_col = jnp.where(below, rest[lo:, k : k + 1] * scale, 0.0)
        l_row = inv_l[k : k + 1, :]
        right = jnp.where(lane > k, s_row, 0.0)
        upper[k : k + 1, :] = s_row
        scales = jnp.where(lane == k, scale, scales)
        work[lo:, :] = work[lo:, :] - c_col * c_row
        inv_c[lo:, :] = jnp.where(rows[lo:] == k, x_row, inv_c[lo:, :] - c_col * x_row)
        rest[lo:, :] = rest[lo:, :] - l_col * right
        inv_l[lo:, :] = inv_l[lo:, :] - l_col * l_row
        s_col = inv_s[:hi, k : k + 1] * scale
        inv_s[:hi, :] = jnp.where(lanes[:hi] == k, s_col, inv_s[:hi, :] - s_col * right)
    lower[...] = jnp.where(rows > lanes, rest[...] * scales, eye)
    tfac[...] = -mm(upper[...], mm(inv_l[...], inv_c[...]), NT)


def update_kernel(vec_rows, vec_cols, got, partner, matrix, tfac, out, moved):
    rows, cols = matrix.shape
    at = lane_ceil(cols + rows)
    core = lax.axis_index("core")
    for part in range(got.shape[0]):
        here = pl.ds(pl.multiple_of((2 * part + core) * SUB, SUB), SUB)
        there = pl.ds(pl.multiple_of((2 * part + 1 - core) * SUB, SUB), SUB)
        moved[here, :cols] = got[part, :, at + NB :]
        moved[here, cols:] = got[part, :, cols : at + NB]
        moved[there, :] = partner[part]
    t = tfac[...]
    mid = mm(t, mm(moved[:, at:], t), TN)
    upd_cols = mm(t, moved[:, :cols], TN) - 0.5 * mm(mid, vec_cols[...])
    upd_rows = mm(t, moved[:, cols : cols + rows], TN) - 0.5 * mm(mid, vec_rows[...])
    left = jnp.concatenate([vec_rows[...], upd_rows], 0)
    right = jnp.concatenate([upd_cols, vec_cols[...]], 0)
    out[...] = matrix[...] - mm(left, right, TN)


def call(kernel, shapes, *args, scratch=(), cost=None):
    outs = [jax.ShapeDtypeStruct(s, jnp.float32) for s in shapes]
    return pl.pallas_call(
        kernel,
        out_shape=outs,
        scratch_shapes=[pltpu.VMEM(s, jnp.float32) for s in scratch],
        compiler_params=pltpu.CompilerParams(vmem_limit_bytes=VMEM_BYTES),
        cost_estimate=cost,
    )(*args)


def exchange(blocks, axis):
    return lax.all_to_all(blocks, axis, 0, 0)


def local(matrix, panel):
    rows, cols = matrix.shape
    n_row, n_chip = lax.axis_size("prow"), lax.axis_size("y")
    n_col = n_chip * lax.axis_size("core")
    block_t = jnp.broadcast_to(panel.T[None], (n_col, SUB, rows))
    rows_t = exchange(block_t, PCOL).reshape(NB, rows)
    (sent,) = call(gram_kernel, [(n_row, SUB, NB + rows)], rows_t)
    small, blocks = call(
        sort_kernel, [(n_col, SUB, 2 * NB), (n_col, SUB, cols)], exchange(sent, "prow")
    )
    band, inv_s, lower, tfac = call(
        factor_kernel,
        [(NB, NB)] * 4,
        exchange(small, PCOL),
        scratch=[(NB, NB)] * 5,
        cost=pl.CostEstimate(flops=2 * 10**10, bytes_accessed=2**20, transcendentals=0),
    )
    cols_t = exchange(blocks, PCOL).reshape(NB, cols)
    vec_rows, vec_cols, sent = call(
        product_kernel,
        [(NB, rows), (NB, cols), (n_col, SUB, rows)],
        rows_t,
        cols_t,
        matrix,
        inv_s,
        lower,
    )
    (sent,) = call(reduce_kernel, [(n_row, SUB, NB + rows)], exchange(sent, PCOL), vec_rows)
    wide = lane_ceil(cols + rows) + NB
    (sent,) = call(spread_kernel, [(n_chip, SUB, wide + cols)], exchange(sent, "prow"))
    got = exchange(sent, "y")
    partner = lax.ppermute(got[:, :, :wide], "core", [(0, 1), (1, 0)])
    (trailing,) = call(
        update_kernel,
        [(rows, cols)],
        vec_rows,
        vec_cols,
        got,
        partner,
        matrix,
        tfac,
        scratch=[(NB, wide)],
    )
    return (trailing, band)


def solution(mesh):
    n_row, n_col = mesh.devices.shape
    grid = Mesh(mesh.devices.reshape(n_row, n_col // 2, 2), ("prow",) + PCOL)
    specs = (P("prow", PCOL), P("prow", PCOL))
    return jax.shard_map(
        local, mesh=grid, in_specs=specs, out_specs=(P("prow", PCOL), P()), check_vma=False
    )
```

```python
import jax
import jax.numpy as jnp
from jax import lax
from jax.experimental import pallas as pl
from jax.experimental.pallas import tpu as pltpu
from jax.sharding import PartitionSpec as P

PRECISE = lax.Precision.HIGHEST
VMEM_BYTES = 48 * 2**20
NB = 128
SUB = 8
HALF = SUB // 2


def mm(left, right, contract=((1,), (0,))):
    return lax.dot_general(
        left, right, (contract, ((), ())), precision=PRECISE, preferred_element_type=jnp.float32
    )


def lane_ceil(count):
    return -(-count // NB) * NB


def halves(block):
    high = block.astype(jnp.bfloat16)
    return high, (block - high.astype(jnp.float32)).astype(jnp.bfloat16)


def mm3(left, right, contract=((1,), (0,))):
    left_high, left_low = halves(left)
    right_high, right_low = halves(right)

    def dot(a, b):
        return lax.dot_general(a, b, (contract, ((), ())), preferred_element_type=jnp.float32)

    return dot(left_high, right_high) + (dot(left_high, right_low) + dot(left_low, right_high))


NT = ((1,), (1,))
TN = ((0,), (0,))


def first_rows_zeroed(block, is_first):
    lanes = lax.broadcasted_iota(jnp.int32, block.shape, 1)
    return jnp.where(is_first & (lanes < NB), 0.0, block)


def gram_kernel(rows_t, sent):
    own = pl.ds(pl.multiple_of(lax.axis_index("pcol") * SUB, SUB), SUB)
    block = rows_t[own, :]
    gram = mm(block, rows_t[...], NT)
    for dest in range(sent.shape[0]):
        sent[dest, :, :NB] = gram
        sent[dest, :, NB:] = block


def sort_kernel(got, small, blocks):
    rows = got.shape[2] - NB
    gram = jnp.sum(got[:, :, :NB], axis=0)
    for dest in range(small.shape[0]):
        small[dest, :, :NB] = gram
        small[dest, :, NB:] = got[0, :, NB : 2 * NB]
        blocks[dest, :, :rows] = got[2 * dest, :, NB:]
        blocks[dest, :, rows:] = got[2 * dest + 1, :, NB:]


def vectors(panel_t, combine, low, is_first):
    vec = mm(combine, first_rows_zeroed(panel_t, is_first), TN)
    head = vec[:, :NB] + low.T * jnp.where(is_first, 1.0, 0.0)
    return jnp.concatenate([head, vec[:, NB:]], 1)


def product_kernel(rows_t, matrix, inv_s, lower, vec_rows, sent):
    vec = vectors(rows_t[...], -inv_s[...], lower[...], lax.axis_index("prow") == 0)
    vec_rows[...] = vec
    part = mm(vec, matrix[...])
    for dest in range(sent.shape[0]):
        sent[dest] = part[dest * HALF : (dest + 1) * HALF]


def column_kernel(cols_t, inv_s, lower, vec_cols):
    vec_cols[...] = vectors(
        cols_t[...], -inv_s[...], lower[...], lax.axis_index("pcol") == 0
    )


def reduce_kernel(got, vec_cols, sent):
    cols = vec_cols.shape[1]
    total = jnp.sum(got[...], axis=0)
    small = mm3(total, vec_cols[...], NT)
    for dest in range(sent.shape[0]):
        sent[dest, :, :cols] = total
        sent[dest, :, cols:] = small


def spread_kernel(got, sent):
    cols = got.shape[2] - NB
    rows = cols // 2
    at = lane_ceil(cols + rows)
    own = got[lax.axis_index("pcol"), :, :cols]
    small = jnp.sum(got[:, :, cols:], axis=0)
    for part in range(got.shape[0]):
        whole = got[part, :, :cols]
        for half in range(2):
            dest = 2 * part + half
            sent[dest, :, :cols] = own
            sent[dest, :, cols : cols + rows] = whole[:, half * rows : (half + 1) * rows]
            sent[dest, :, cols + rows : at] = jnp.zeros((HALF, at - cols - rows), jnp.float32)
            sent[dest, :, at:] = small


def factor_kernel(got, band, inv_s, lower, tfac, work, inv_c, rest, inv_l, upper):
    rows = lax.broadcasted_iota(jnp.int32, (NB, NB), 0)
    lanes = lax.broadcasted_iota(jnp.int32, (NB, NB), 1)
    lane = lax.broadcasted_iota(jnp.int32, (1, NB), 1)
    eye = jnp.where(rows == lanes, 1.0, 0.0)
    for part in range(got.shape[0]):
        work[part * SUB : (part + 1) * SUB, :] = got[part, :, :NB]
        rest[part * SUB : (part + 1) * SUB, :] = -got[part, :, NB:]
    rest[...] = rest[...].T
    inv_c[...] = eye
    inv_l[...] = eye
    inv_s[...] = eye
    scales = jnp.zeros((1, NB), jnp.float32)
    for k in range(NB):
        lo = (k // SUB) * SUB
        hi = lo + SUB
        below = rows[lo:, :1] > k
        inv = lax.rsqrt(work[k : k + 1, k : k + 1])
        c_row = jnp.where(lane >= k, work[k : k + 1, :] * inv, 0.0)
        band[k : k + 1, :] = -c_row
        c_col = jnp.where(below, work[lo:, k : k + 1] * inv, 0.0)
        x_row = inv_c[k : k + 1, :] * inv
        s_row = jnp.where(lane >= k, rest[k : k + 1, :] - c_row, 0.0)
        scale = 1.0 / (rest[k : k + 1, k : k + 1] - c_row[:, k : k + 1])
        l_col = jnp.where(below, rest[lo:, k : k + 1] * scale, 0.0)
        l_row = inv_l[k : k + 1, :]
        right = jnp.where(lane > k, s_row, 0.0)
        upper[k : k + 1, :] = s_row
        scales = jnp.where(lane == k, scale, scales)
        work[lo:, :] = work[lo:, :] - c_col * c_row
        inv_c[lo:, :] = jnp.where(rows[lo:] == k, x_row, inv_c[lo:, :] - c_col * x_row)
        rest[lo:, :] = rest[lo:, :] - l_col * right
        inv_l[lo:, :] = inv_l[lo:, :] - l_col * l_row
        s_col = inv_s[:hi, k : k + 1] * scale
        inv_s[:hi, :] = jnp.where(lanes[:hi] == k, s_col, inv_s[:hi, :] - s_col * right)
    lower[...] = jnp.where(rows > lanes, rest[...] * scales, eye)
    tfac[...] = -mm(upper[...], mm(inv_l[...], inv_c[...]), NT)


def update_kernel(vec_rows, vec_cols, got, matrix, tfac, out, moved):
    rows, cols = matrix.shape
    at = lane_ceil(cols + rows)
    for part in range(got.shape[0]):
        moved[part * HALF : (part + 1) * HALF, :] = got[part]
    t = tfac[...]
    mid = mm3(t, mm3(moved[:, at:], t), TN)
    prod = mm3(t, moved[:, : cols + rows], TN)
    upd_cols = prod[:, :cols] - mm3(0.5 * (mid + mid.T), vec_cols[...])
    left = jnp.concatenate([vec_rows[...], prod[:, cols:]], 0)
    right = jnp.concatenate([upd_cols, vec_cols[...]], 0)
    out[...] = matrix[...] - mm3(left, right, TN)


def call(kernel, shapes, *args, scratch=(), cost=None):
    outs = [jax.ShapeDtypeStruct(s, jnp.float32) for s in shapes]
    return pl.pallas_call(
        kernel,
        out_shape=outs,
        scratch_shapes=[pltpu.VMEM(s, jnp.float32) for s in scratch],
        compiler_params=pltpu.CompilerParams(vmem_limit_bytes=VMEM_BYTES),
        cost_estimate=cost,
    )(*args)


def exchange(blocks, axis):
    return lax.all_to_all(blocks, axis, 0, 0)


def local(matrix, panel):
    rows, cols = matrix.shape
    n_row, n_col = lax.axis_size("prow"), lax.axis_size("pcol")
    block_t = jnp.broadcast_to(panel.T[None], (n_col, SUB, rows))
    rows_t = exchange(block_t, "pcol").reshape(NB, rows)
    (sent,) = call(gram_kernel, [(n_row, SUB, NB + rows)], rows_t)
    small, blocks = call(
        sort_kernel, [(n_col, SUB, 2 * NB), (n_col, SUB, cols)], exchange(sent, "prow")
    )
    band, inv_s, lower, tfac = call(
        factor_kernel,
        [(NB, NB)] * 4,
        exchange(small, "pcol"),
        scratch=[(NB, NB)] * 5,
        cost=pl.CostEstimate(flops=2 * 10**10, bytes_accessed=2**20, transcendentals=0),
    )
    cols_t = exchange(blocks, "pcol").reshape(NB, cols)
    vec_rows, sent = call(
        product_kernel, [(NB, rows), (n_row, HALF, cols)], rows_t, matrix, inv_s, lower
    )
    (vec_cols,) = call(column_kernel, [(NB, cols)], cols_t, inv_s, lower)
    (sent,) = call(
        reduce_kernel, [(n_col, HALF, cols + NB)], exchange(sent, "prow"), vec_cols
    )
    wide = lane_ceil(cols + rows) + NB
    (sent,) = call(spread_kernel, [(n_row, HALF, wide)], exchange(sent, "pcol"))
    (trailing,) = call(
        update_kernel,
        [(rows, cols)],
        vec_rows,
        vec_cols,
        exchange(sent, "prow"),
        matrix,
        tfac,
        scratch=[(NB, wide)],
    )
    return (trailing, band)


def solution(mesh):
    specs = (P("prow", "pcol"), P("prow", "pcol"))
    return jax.shard_map(
        local, mesh=mesh, in_specs=specs, out_specs=(P("prow", "pcol"), P()), check_vma=False
    )
```

```python
import jax
import jax.numpy as jnp
from jax import lax
from jax.experimental import pallas as pl
from jax.experimental.pallas import tpu as pltpu
from jax.sharding import PartitionSpec as P

PRECISE = lax.Precision.HIGHEST
VMEM_BYTES = 48 * 2**20
NB = 128
SUB = 8
HALF = SUB // 2


def mm(left, right, contract=((1,), (0,))):
    return lax.dot_general(
        left, right, (contract, ((), ())), precision=PRECISE, preferred_element_type=jnp.float32
    )


def lane_ceil(count):
    return -(-count // NB) * NB


def halves(block):
    high = block.astype(jnp.bfloat16)
    return high, (block - high.astype(jnp.float32)).astype(jnp.bfloat16)


def mm3(left, right, contract=((1,), (0,))):
    left_high, left_low = halves(left)
    right_high, right_low = halves(right)

    def dot(a, b):
        return lax.dot_general(a, b, (contract, ((), ())), preferred_element_type=jnp.float32)

    return dot(left_high, right_high) + (dot(left_high, right_low) + dot(left_low, right_high))


NT = ((1,), (1,))
TN = ((0,), (0,))


def first_rows_zeroed(block, is_first):
    lanes = lax.broadcasted_iota(jnp.int32, block.shape, 1)
    return jnp.where(is_first & (lanes < NB), 0.0, block)


def gram_kernel(rows_t, sent):
    j = lax.axis_index("pcol")
    own = pl.ds(pl.multiple_of(j * SUB, SUB), SUB)
    block = rows_t[own, :]
    gram = mm(block, rows_t[...], NT)
    first = rows_t[:SUB, :NB]
    extra = jnp.where(j == 1, first[:HALF], first[HALF:])
    pad = jnp.zeros((HALF, rows_t.shape[1] - 3 * NB), jnp.float32)
    top = jnp.concatenate([block[:HALF, :NB], block[HALF:, :NB], extra, pad], 1)
    use_top = (lax.axis_index("prow") == 0) & (j > 0)
    for dest in range(sent.shape[0]):
        sent[dest, :, :NB] = gram[:HALF]
        sent[dest, :, NB : 2 * NB] = gram[HALF:]
        piece = rows_t[dest * HALF : (dest + 1) * HALF, :]
        sent[dest, :, 2 * NB :] = jnp.where(use_top, top, piece)


def sort_kernel(got, small, blocks):
    j = lax.axis_index("pcol")
    gram = jnp.sum(got[:, :, : 2 * NB], axis=0)
    top = got[0, :, 2 * NB : 5 * NB]
    left = got[2 * j, :, 2 * NB :]
    right = got[2 * j + 1, :, 2 * NB :]
    both = jnp.concatenate([left, right], 1)
    for dest in range(small.shape[0]):
        small[dest, :, : 2 * NB] = gram
        small[dest, :, 2 * NB :] = top
    for dest in range(blocks.shape[0]):
        blocks[dest] = both


def vectors(panel_t, combine, low, is_first):
    vec = mm(combine, first_rows_zeroed(panel_t, is_first), TN)
    head = vec[:, :NB] + low.T * jnp.where(is_first, 1.0, 0.0)
    return jnp.concatenate([head, vec[:, NB:]], 1)


def product_kernel(rows_t, matrix, inv_s, lower, vec_rows, sent):
    vec = vectors(rows_t[...], -inv_s[...], lower[...], lax.axis_index("prow") == 0)
    vec_rows[...] = vec
    part = mm(vec, matrix[...])
    for dest in range(sent.shape[0]):
        sent[dest] = part[dest * HALF : (dest + 1) * HALF]


def column_kernel(got, inv_s, lower, vec_cols, cols_t):
    for part in range(got.shape[0]):
        cols_t[part * HALF : (part + 1) * HALF, :] = got[part]
    vec_cols[...] = vectors(
        cols_t[...], -inv_s[...], lower[...], lax.axis_index("pcol") == 0
    )


def reduce_kernel(got, vec_cols, sent):
    cols = vec_cols.shape[1]
    total = jnp.sum(got[...], axis=0)
    small = mm3(total, vec_cols[...], NT)
    for dest in range(sent.shape[0]):
        sent[dest, :, :cols] = total
        sent[dest, :, cols:] = small


def spread_kernel(got, sent):
    cols = got.shape[2] - NB
    rows = cols // 2
    at = lane_ceil(cols + rows)
    own = got[lax.axis_index("pcol"), :, :cols]
    small = jnp.sum(got[:, :, cols:], axis=0)
    for part in range(got.shape[0]):
        whole = got[part, :, :cols]
        for half in range(2):
            dest = 2 * part + half
            sent[dest, :, :cols] = own
            sent[dest, :, cols : cols + rows] = whole[:, half * rows : (half + 1) * rows]
            sent[dest, :, cols + rows : at] = jnp.zeros((HALF, at - cols - rows), jnp.float32)
            sent[dest, :, at:] = small


def factor_kernel(got, band, inv_s, lower, tfac, work, inv_c, rest, inv_l, upper):
    rows = lax.broadcasted_iota(jnp.int32, (NB, NB), 0)
    lanes = lax.broadcasted_iota(jnp.int32, (NB, NB), 1)
    lane = lax.broadcasted_iota(jnp.int32, (1, NB), 1)
    eye = jnp.where(rows == lanes, 1.0, 0.0)
    for part in range(got.shape[0]):
        for half in range(2):
            to = slice(part * SUB + half * HALF, part * SUB + (half + 1) * HALF)
            work[to, :] = got[part, :, half * NB : (half + 1) * NB]
            source, at = (half + 1, 4) if part == 0 else (part, 2 + half)
            rest[to, :] = -got[source, :, at * NB : (at + 1) * NB]
    rest[...] = rest[...].T
    inv_c[...] = eye
    inv_l[...] = eye
    inv_s[...] = eye
    scales = jnp.zeros((1, NB), jnp.float32)
    for k in range(NB):
        lo = (k // SUB) * SUB
        hi = lo + SUB
        below = rows[lo:, :1] > k
        inv = lax.rsqrt(work[k : k + 1, k : k + 1])
        c_row = jnp.where(lane >= k, work[k : k + 1, :] * inv, 0.0)
        band[k : k + 1, :] = -c_row
        c_col = jnp.where(below, work[lo:, k : k + 1] * inv, 0.0)
        x_row = inv_c[k : k + 1, :] * inv
        s_row = jnp.where(lane >= k, rest[k : k + 1, :] - c_row, 0.0)
        scale = 1.0 / (rest[k : k + 1, k : k + 1] - c_row[:, k : k + 1])
        l_col = jnp.where(below, rest[lo:, k : k + 1] * scale, 0.0)
        l_row = inv_l[k : k + 1, :]
        right = jnp.where(lane > k, s_row, 0.0)
        upper[k : k + 1, :] = s_row
        scales = jnp.where(lane == k, scale, scales)
        work[lo:, :] = work[lo:, :] - c_col * c_row
        inv_c[lo:, :] = jnp.where(rows[lo:] == k, x_row, inv_c[lo:, :] - c_col * x_row)
        rest[lo:, :] = rest[lo:, :] - l_col * right
        inv_l[lo:, :] = inv_l[lo:, :] - l_col * l_row
        s_col = inv_s[:hi, k : k + 1] * scale
        inv_s[:hi, :] = jnp.where(lanes[:hi] == k, s_col, inv_s[:hi, :] - s_col * right)
    lower[...] = jnp.where(rows > lanes, rest[...] * scales, eye)
    tfac[...] = -mm(upper[...], mm(inv_l[...], inv_c[...]), NT)


def update_kernel(vec_rows, vec_cols, got, matrix, tfac, out, moved):
    rows, cols = matrix.shape
    at = lane_ceil(cols + rows)
    for part in range(got.shape[0]):
        moved[part * HALF : (part + 1) * HALF, :] = got[part]
    t = tfac[...]
    mid = mm3(t, mm3(moved[:, at:], t), TN)
    prod = mm3(t, moved[:, : cols + rows], TN)
    upd_cols = prod[:, :cols] - mm3(0.5 * (mid + mid.T), vec_cols[...])
    left = jnp.concatenate([vec_rows[...], prod[:, cols:]], 0)
    right = jnp.concatenate([upd_cols, vec_cols[...]], 0)
    out[...] = matrix[...] - mm3(left, right, TN)


def call(kernel, shapes, *args, scratch=(), cost=None):
    outs = [jax.ShapeDtypeStruct(s, jnp.float32) for s in shapes]
    return pl.pallas_call(
        kernel,
        out_shape=outs,
        scratch_shapes=[pltpu.VMEM(s, jnp.float32) for s in scratch],
        compiler_params=pltpu.CompilerParams(vmem_limit_bytes=VMEM_BYTES),
        cost_estimate=cost,
    )(*args)


def exchange(blocks, axis):
    return lax.all_to_all(blocks, axis, 0, 0)


def local(matrix, panel):
    rows, cols = matrix.shape
    n_row, n_col = lax.axis_size("prow"), lax.axis_size("pcol")
    block_t = jnp.broadcast_to(panel.T[None], (n_col, SUB, rows))
    rows_t = exchange(block_t, "pcol").reshape(NB, rows)
    (sent,) = call(gram_kernel, [(n_row, HALF, 2 * NB + rows)], rows_t)
    small, blocks = call(
        sort_kernel, [(n_col, HALF, 5 * NB), (n_row, HALF, cols)], exchange(sent, "prow")
    )
    band, inv_s, lower, tfac = call(
        factor_kernel,
        [(NB, NB)] * 4,
        exchange(small, "pcol"),
        scratch=[(NB, NB)] * 5,
        cost=pl.CostEstimate(flops=2 * 10**10, bytes_accessed=2**20, transcendentals=0),
    )
    cols_t = exchange(blocks, "prow")
    vec_rows, sent = call(
        product_kernel, [(NB, rows), (n_row, HALF, cols)], rows_t, matrix, inv_s, lower
    )
    (vec_cols,) = call(
        column_kernel, [(NB, cols)], cols_t, inv_s, lower, scratch=[(NB, cols)]
    )
    (sent,) = call(
        reduce_kernel, [(n_col, HALF, cols + NB)], exchange(sent, "prow"), vec_cols
    )
    wide = lane_ceil(cols + rows) + NB
    (sent,) = call(spread_kernel, [(n_row, HALF, wide)], exchange(sent, "pcol"))
    (trailing,) = call(
        update_kernel,
        [(rows, cols)],
        vec_rows,
        vec_cols,
        exchange(sent, "prow"),
        matrix,
        tfac,
        scratch=[(NB, wide)],
    )
    return (trailing, band)


def solution(mesh):
    specs = (P("prow", "pcol"), P("prow", "pcol"))
    return jax.shard_map(
        local, mesh=mesh, in_specs=specs, out_specs=(P("prow", "pcol"), P()), check_vma=False
    )
```

```python
import jax
import jax.numpy as jnp
from jax import lax
from jax.experimental import pallas as pl
from jax.experimental.pallas import tpu as pltpu
from jax.sharding import PartitionSpec as P

PRECISE = lax.Precision.HIGHEST
VMEM_BYTES = 24 * 2**20
NB = 128
SUB = 8
HALF = SUB // 2
STEP = 4


def mm(left, right, contract=((1,), (0,))):
    return lax.dot_general(
        left, right, (contract, ((), ())), precision=PRECISE, preferred_element_type=jnp.float32
    )


def lane_ceil(count):
    return -(-count // NB) * NB


def halves(block):
    high = block.astype(jnp.bfloat16)
    return high, (block - high.astype(jnp.float32)).astype(jnp.bfloat16)


def mm3(left, right, contract=((1,), (0,))):
    left_high, left_low = halves(left)
    right_high, right_low = halves(right)

    def dot(a, b):
        return lax.dot_general(a, b, (contract, ((), ())), preferred_element_type=jnp.float32)

    return dot(left_high, right_high) + (dot(left_high, right_low) + dot(left_low, right_high))


NT = ((1,), (1,))
TN = ((0,), (0,))


def first_rows_zeroed(block, is_first):
    lanes = lax.broadcasted_iota(jnp.int32, block.shape, 1)
    return jnp.where(is_first & (lanes < NB), 0.0, block)


def gram_kernel(rows_t, sent):
    j = lax.axis_index("pcol")
    own = pl.ds(pl.multiple_of(j * SUB, SUB), SUB)
    block = rows_t[own, :]
    gram = mm(block, rows_t[...], NT)
    first = rows_t[:SUB, :NB]
    extra = jnp.where(j == 1, first[:HALF], first[HALF:])
    pad = jnp.zeros((HALF, rows_t.shape[1] - 3 * NB), jnp.float32)
    top = jnp.concatenate([block[:HALF, :NB], block[HALF:, :NB], extra, pad], 1)
    use_top = (lax.axis_index("prow") == 0) & (j > 0)
    for dest in range(sent.shape[0]):
        sent[dest, :, :NB] = gram[:HALF]
        sent[dest, :, NB : 2 * NB] = gram[HALF:]
        piece = rows_t[dest * HALF : (dest + 1) * HALF, :]
        sent[dest, :, 2 * NB :] = jnp.where(use_top, top, piece)


def sort_kernel(got, small, blocks):
    j = lax.axis_index("pcol")
    gram = jnp.sum(got[:, :, : 2 * NB], axis=0)
    top = got[0, :, 2 * NB : 5 * NB]
    left = got[2 * j, :, 2 * NB :]
    right = got[2 * j + 1, :, 2 * NB :]
    both = jnp.concatenate([left, right], 1)
    for dest in range(small.shape[0]):
        small[dest, :, : 2 * NB] = gram
        small[dest, :, 2 * NB :] = top
    for dest in range(blocks.shape[0]):
        blocks[dest] = both


def vectors(panel_t, combine, low, is_first):
    vec = mm(combine, first_rows_zeroed(panel_t, is_first), TN)
    head = vec[:, :NB] + low.T * jnp.where(is_first, 1.0, 0.0)
    return jnp.concatenate([head, vec[:, NB:]], 1)


def product_kernel(rows_t, matrix, inv_s, lower, vec_rows, sent):
    vec = vectors(rows_t[...], -inv_s[...], lower[...], lax.axis_index("prow") == 0)
    vec_rows[...] = vec
    part = mm(vec, matrix[...])
    for dest in range(sent.shape[0]):
        sent[dest] = part[dest * HALF : (dest + 1) * HALF]


def column_kernel(got, inv_s, lower, vec_cols, cols_t):
    for part in range(got.shape[0]):
        cols_t[part * HALF : (part + 1) * HALF, :] = got[part]
    vec_cols[...] = vectors(
        cols_t[...], -inv_s[...], lower[...], lax.axis_index("pcol") == 0
    )


def reduce_kernel(got, vec_cols, sent):
    cols = vec_cols.shape[1]
    total = jnp.sum(got[...], axis=0)
    small = mm3(total, vec_cols[...], NT)
    for dest in range(sent.shape[0]):
        sent[dest, :, :cols] = total
        sent[dest, :, cols:] = small


def spread_kernel(got, sent):
    cols = got.shape[2] - NB
    rows = cols // 2
    at = lane_ceil(cols + rows)
    own = got[lax.axis_index("pcol"), :, :cols]
    small = jnp.sum(got[:, :, cols:], axis=0)
    for part in range(got.shape[0]):
        whole = got[part, :, :cols]
        for half in range(2):
            dest = 2 * part + half
            sent[dest, :, :cols] = own
            sent[dest, :, cols : cols + rows] = whole[:, half * rows : (half + 1) * rows]
            sent[dest, :, cols + rows : at] = jnp.zeros((HALF, at - cols - rows), jnp.float32)
            sent[dest, :, at:] = small


def factor_kernel(got, band, inv_s, lower, tfac, work, inv_c, rest, inv_l, upper):
    rows = lax.broadcasted_iota(jnp.int32, (NB, NB), 0)
    lanes = lax.broadcasted_iota(jnp.int32, (NB, NB), 1)
    lane = lax.broadcasted_iota(jnp.int32, (1, NB), 1)
    eye = jnp.where(rows == lanes, 1.0, 0.0)
    for part in range(got.shape[0]):
        for half in range(2):
            to = slice(part * SUB + half * HALF, part * SUB + (half + 1) * HALF)
            work[to, :] = got[part, :, half * NB : (half + 1) * NB]
            source, at = (half + 1, 4) if part == 0 else (part, 2 + half)
            rest[to, :] = -got[source, :, at * NB : (at + 1) * NB]
    rest[...] = rest[...].T
    for ref in (inv_c, inv_l, inv_s, lower):
        ref[...] = eye

    def spread(column):
        return jnp.broadcast_to(column, (column.shape[0], NB))

    for first in range(0, NB, STEP):
        lo = first // SUB * SUB
        hi = lo + SUB
        block = range(first, first + STEP)
        row_at = rows[lo:]
        gram_col = [spread(work[lo:, k : k + 1]) for k in block]
        rest_col = [spread(rest[lo:, k : k + 1]) for k in block]
        inv_col = [spread(inv_s[:hi, k : k + 1]) for k in block]
        gram_row = [work[k : k + 1, :] for k in block]
        rest_row = [rest[k : k + 1, :] for k in block]
        c_inv_row = [inv_c[k : k + 1, :] for k in block]
        l_inv_row = [inv_l[k : k + 1, :] for k in block]
        done = []
        for t, k in enumerate(block):
            here = slice(k - lo, k - lo + 1)
            pivot = gram_col[t][here]
            inv = lax.rsqrt(pivot)
            c_col = jnp.where(row_at > k, gram_col[t] * inv, 0.0)
            c_row = jnp.where(lane >= k, gram_row[t] * inv, 0.0)
            x_row = c_inv_row[t] * inv
            s_row = jnp.where(lane >= k, rest_row[t] - c_row, 0.0)
            scale = 1.0 / (rest_col[t][here] - pivot * inv)
            l_col = jnp.where(row_at > k, rest_col[t] * scale, 0.0)
            right = jnp.where(lane > k, s_row, 0.0)
            x_col = inv_col[t] * scale
            l_row = l_inv_row[t]
            band[k : k + 1, :] = -c_row
            upper[k : k + 1, :] = s_row
            for u in range(t + 1, STEP):
                there = slice(first + u - lo, first + u - lo + 1)
                c, l = c_col[there], l_col[there]
                s = rest_col[u][here] - c
                gram_col[u] = gram_col[u] - c_col * c
                rest_col[u] = rest_col[u] - l_col * s
                inv_col[u] = inv_col[u] - x_col * s
                gram_row[u] = gram_row[u] - c * c_row
                c_inv_row[u] = c_inv_row[u] - c * x_row
                rest_row[u] = rest_row[u] - l * right
                l_inv_row[u] = l_inv_row[u] - l * l_row
            done.append((c_col, c_row, x_row, l_col, l_row, right, x_col))
        below = (first + STEP) // SUB * SUB
        if below < NB:
            for ref, col, row in ((work, 0, 1), (rest, 3, 5), (inv_c, 0, 2), (inv_l, 3, 4)):
                total = ref[below:, :]
                for terms in done:
                    total = total - terms[col][below - lo :] * terms[row]
                ref[below:, :] = total
        above = inv_s[:hi, :]
        for terms in done:
            above = above - terms[6] * terms[5]
        low = lower[lo:, :]
        for k, terms in zip(block, done):
            above = jnp.where(lanes[:hi] == k, terms[6], above)
            low = jnp.where((lanes[lo:] == k) & (row_at > k), terms[3], low)
            inv_c[k : k + 1, :] = terms[2]
            inv_l[k : k + 1, :] = terms[4]
        inv_s[:hi, :] = above
        lower[lo:, :] = low
    tfac[...] = -mm(upper[...], mm(inv_l[...], inv_c[...]), NT)


def update_kernel(vec_rows, vec_cols, got, matrix, tfac, out, moved):
    rows, cols = matrix.shape
    at = lane_ceil(cols + rows)
    for part in range(got.shape[0]):
        moved[part * HALF : (part + 1) * HALF, :] = got[part]
    t = tfac[...]
    mid = mm3(t, mm3(moved[:, at:], t), TN)
    prod = mm3(t, moved[:, : cols + rows], TN)
    upd_cols = prod[:, :cols] - mm3(0.5 * (mid + mid.T), vec_cols[...])
    left = jnp.concatenate([vec_rows[...], prod[:, cols:]], 0)
    right = jnp.concatenate([upd_cols, vec_cols[...]], 0)
    out[...] = matrix[...] - mm3(left, right, TN)


def call(kernel, shapes, *args, scratch=(), cost=None, vmem=VMEM_BYTES):
    outs = [jax.ShapeDtypeStruct(s, jnp.float32) for s in shapes]
    return pl.pallas_call(
        kernel,
        out_shape=outs,
        scratch_shapes=[pltpu.VMEM(s, jnp.float32) for s in scratch],
        compiler_params=pltpu.CompilerParams(vmem_limit_bytes=vmem),
        cost_estimate=cost,
    )(*args)


def exchange(blocks, axis):
    return lax.all_to_all(blocks, axis, 0, 0)


def local(matrix, panel):
    rows, cols = matrix.shape
    n_row, n_col = lax.axis_size("prow"), lax.axis_size("pcol")
    block_t = jnp.broadcast_to(panel.T[None], (n_col, SUB, rows))
    rows_t = exchange(block_t, "pcol").reshape(NB, rows)
    (sent,) = call(gram_kernel, [(n_row, HALF, 2 * NB + rows)], rows_t)
    small, blocks = call(
        sort_kernel, [(n_col, HALF, 5 * NB), (n_row, HALF, cols)], exchange(sent, "prow")
    )
    band, inv_s, lower, tfac = call(
        factor_kernel,
        [(NB, NB)] * 4,
        exchange(small, "pcol"),
        scratch=[(NB, NB)] * 5,
        cost=pl.CostEstimate(flops=2 * 10**10, bytes_accessed=2**20, transcendentals=0),
        vmem=8 * 2**20,
    )
    cols_t = exchange(blocks, "prow")
    vec_rows, sent = call(
        product_kernel, [(NB, rows), (n_row, HALF, cols)], rows_t, matrix, inv_s, lower
    )
    (vec_cols,) = call(
        column_kernel, [(NB, cols)], cols_t, inv_s, lower, scratch=[(NB, cols)]
    )
    (sent,) = call(
        reduce_kernel, [(n_col, HALF, cols + NB)], exchange(sent, "prow"), vec_cols
    )
    wide = lane_ceil(cols + rows) + NB
    (sent,) = call(spread_kernel, [(n_row, HALF, wide)], exchange(sent, "pcol"))
    (trailing,) = call(
        update_kernel,
        [(rows, cols)],
        vec_rows,
        vec_cols,
        exchange(sent, "prow"),
        matrix,
        tfac,
        scratch=[(NB, wide)],
    )
    return (trailing, band)


def solution(mesh):
    specs = (P("prow", "pcol"), P("prow", "pcol"))
    return jax.shard_map(
        local, mesh=mesh, in_specs=specs, out_specs=(P("prow", "pcol"), P()), check_vma=False
    )
```

```python
import jax
import jax.numpy as jnp
from jax import lax
from jax.experimental import pallas as pl
from jax.experimental.pallas import tpu as pltpu
from jax.sharding import PartitionSpec as P

PRECISE = lax.Precision.HIGHEST
VMEM_BYTES = 24 * 2**20
NB = 128
SUB = 8
HALF = SUB // 2
STEP = 4


def mm(left, right, contract=((1,), (0,))):
    return lax.dot_general(
        left, right, (contract, ((), ())), precision=PRECISE, preferred_element_type=jnp.float32
    )


def lane_ceil(count):
    return -(-count // NB) * NB


def halves(block):
    high = block.astype(jnp.bfloat16)
    return high, (block - high.astype(jnp.float32)).astype(jnp.bfloat16)


def mm3(left, right, contract=((1,), (0,))):
    left_high, left_low = halves(left)
    right_high, right_low = halves(right)

    def dot(a, b):
        return lax.dot_general(a, b, (contract, ((), ())), preferred_element_type=jnp.float32)

    return dot(left_high, right_high) + (dot(left_high, right_low) + dot(left_low, right_high))


NT = ((1,), (1,))
TN = ((0,), (0,))


def first_rows_zeroed(block, is_first):
    lanes = lax.broadcasted_iota(jnp.int32, block.shape, 1)
    return jnp.where(is_first & (lanes < NB), 0.0, block)


def gram_kernel(rows_t, sent):
    j = lax.axis_index("pcol")
    own = pl.ds(pl.multiple_of(j * SUB, SUB), SUB)
    block = rows_t[own, :]
    gram = mm(block, rows_t[...], NT)
    first = rows_t[:SUB, :NB]
    extra = jnp.where(j == 1, first[:HALF], first[HALF:])
    pad = jnp.zeros((HALF, rows_t.shape[1] - 3 * NB), jnp.float32)
    top = jnp.concatenate([block[:HALF, :NB], block[HALF:, :NB], extra, pad], 1)
    use_top = (lax.axis_index("prow") == 0) & (j > 0)
    for dest in range(sent.shape[0]):
        sent[dest, :, :NB] = gram[:HALF]
        sent[dest, :, NB : 2 * NB] = gram[HALF:]
        piece = rows_t[dest * HALF : (dest + 1) * HALF, :]
        sent[dest, :, 2 * NB :] = jnp.where(use_top, top, piece)


def sort_kernel(got, small, blocks):
    j = lax.axis_index("pcol")
    gram = jnp.sum(got[:, :, : 2 * NB], axis=0)
    top = got[0, :, 2 * NB : 5 * NB]
    left = got[2 * j, :, 2 * NB :]
    right = got[2 * j + 1, :, 2 * NB :]
    both = jnp.concatenate([left, right], 1)
    for dest in range(small.shape[0]):
        small[dest, :, : 2 * NB] = gram
        small[dest, :, 2 * NB :] = top
    blocks[...] = both


def vectors(panel_t, combine, low, is_first):
    vec = mm(combine, first_rows_zeroed(panel_t, is_first), TN)
    head = vec[:, :NB] + low.T * jnp.where(is_first, 1.0, 0.0)
    return jnp.concatenate([head, vec[:, NB:]], 1)


def product_kernel(rows_t, blocks, matrix, inv_s, lower, vec_rows, sent):
    vec = vectors(rows_t[...], -inv_s[...], lower[...], lax.axis_index("prow") == 0)
    vec_rows[...] = vec
    part = mm(vec, matrix[...])
    block = blocks[...]
    for dest in range(sent.shape[0]):
        sent[dest, :HALF, :] = part[dest * HALF : (dest + 1) * HALF]
        sent[dest, HALF:, :] = block


def reduce_kernel(got, inv_s, lower, vec_cols, sent, cols_t):
    cols = vec_cols.shape[1]
    for part in range(got.shape[0]):
        cols_t[part * HALF : (part + 1) * HALF, :] = got[part, HALF:, :]
    vec = vectors(cols_t[...], -inv_s[...], lower[...], lax.axis_index("pcol") == 0)
    vec_cols[...] = vec
    total = jnp.sum(got[...], axis=0)[:HALF]
    small = mm3(total, vec, NT)
    for dest in range(sent.shape[0]):
        sent[dest, :, :cols] = total
        sent[dest, :, cols:] = small


def spread_kernel(got, sent):
    cols = got.shape[2] - NB
    rows = cols // 2
    at = lane_ceil(cols + rows)
    own = got[lax.axis_index("pcol"), :, :cols]
    small = jnp.sum(got[:, :, cols:], axis=0)
    for part in range(got.shape[0]):
        whole = got[part, :, :cols]
        for half in range(2):
            dest = 2 * part + half
            sent[dest, :, :cols] = own
            sent[dest, :, cols : cols + rows] = whole[:, half * rows : (half + 1) * rows]
            sent[dest, :, cols + rows : at] = jnp.zeros((HALF, at - cols - rows), jnp.float32)
            sent[dest, :, at:] = small


def factor_kernel(got, band, inv_s, lower, tfac, work, inv_c, rest, inv_l, upper):
    rows = lax.broadcasted_iota(jnp.int32, (NB, NB), 0)
    lanes = lax.broadcasted_iota(jnp.int32, (NB, NB), 1)
    lane = lax.broadcasted_iota(jnp.int32, (1, NB), 1)
    eye = jnp.where(rows == lanes, 1.0, 0.0)
    for part in range(got.shape[0]):
        for half in range(2):
            to = slice(part * SUB + half * HALF, part * SUB + (half + 1) * HALF)
            work[to, :] = got[part, :, half * NB : (half + 1) * NB]
            source, at = (half + 1, 4) if part == 0 else (part, 2 + half)
            rest[to, :] = -got[source, :, at * NB : (at + 1) * NB]
    rest[...] = rest[...].T
    for ref in (inv_c, inv_l, inv_s, lower):
        ref[...] = eye

    def spread(column):
        return jnp.broadcast_to(column, (column.shape[0], NB))

    for first in range(0, NB, STEP):
        lo = first // SUB * SUB
        hi = lo + SUB
        block = range(first, first + STEP)
        row_at = rows[lo:]
        gram_col = [spread(work[lo:, k : k + 1]) for k in block]
        rest_col = [spread(rest[lo:, k : k + 1]) for k in block]
        inv_col = [spread(inv_s[:hi, k : k + 1]) for k in block]
        gram_row = [work[k : k + 1, :] for k in block]
        rest_row = [rest[k : k + 1, :] for k in block]
        c_inv_row = [inv_c[k : k + 1, :] for k in block]
        l_inv_row = [inv_l[k : k + 1, :] for k in block]
        done = []
        for t, k in enumerate(block):
            here = slice(k - lo, k - lo + 1)
            pivot = gram_col[t][here]
            inv = lax.rsqrt(pivot)
            c_col = jnp.where(row_at > k, gram_col[t] * inv, 0.0)
            c_row = jnp.where(lane >= k, gram_row[t] * inv, 0.0)
            x_row = c_inv_row[t] * inv
            s_row = jnp.where(lane >= k, rest_row[t] - c_row, 0.0)
            scale = 1.0 / (rest_col[t][here] - pivot * inv)
            l_col = jnp.where(row_at > k, rest_col[t] * scale, 0.0)
            right = jnp.where(lane > k, s_row, 0.0)
            x_col = inv_col[t] * scale
            l_row = l_inv_row[t]
            band[k : k + 1, :] = -c_row
            upper[k : k + 1, :] = s_row
            for u in range(t + 1, STEP):
                there = slice(first + u - lo, first + u - lo + 1)
                c, l = c_col[there], l_col[there]
                s = rest_col[u][here] - c
                gram_col[u] = gram_col[u] - c_col * c
                rest_col[u] = rest_col[u] - l_col * s
                inv_col[u] = inv_col[u] - x_col * s
                gram_row[u] = gram_row[u] - c * c_row
                c_inv_row[u] = c_inv_row[u] - c * x_row
                rest_row[u] = rest_row[u] - l * right
                l_inv_row[u] = l_inv_row[u] - l * l_row
            done.append((c_col, c_row, x_row, l_col, l_row, right, x_col))
        below = (first + STEP) // SUB * SUB
        if below < NB:
            for ref, col, row in ((work, 0, 1), (rest, 3, 5), (inv_c, 0, 2), (inv_l, 3, 4)):
                total = ref[below:, :]
                for terms in done:
                    total = total - terms[col][below - lo :] * terms[row]
                ref[below:, :] = total
        above = inv_s[:hi, :]
        for terms in done:
            above = above - terms[6] * terms[5]
        low = lower[lo:, :]
        for k, terms in zip(block, done):
            above = jnp.where(lanes[:hi] == k, terms[6], above)
            low = jnp.where((lanes[lo:] == k) & (row_at > k), terms[3], low)
            inv_c[k : k + 1, :] = terms[2]
            inv_l[k : k + 1, :] = terms[4]
        inv_s[:hi, :] = above
        lower[lo:, :] = low
    tfac[...] = -mm(upper[...], mm(inv_l[...], inv_c[...]), NT)


def update_kernel(vec_rows, vec_cols, got, matrix, tfac, out, moved):
    rows, cols = matrix.shape
    at = lane_ceil(cols + rows)
    for part in range(got.shape[0]):
        moved[part * HALF : (part + 1) * HALF, :] = got[part]
    t = tfac[...]
    mid = mm3(t, mm3(moved[:, at:], t), TN)
    prod = mm3(t, moved[:, : cols + rows], TN)
    upd_cols = prod[:, :cols] - mm3(0.5 * (mid + mid.T), vec_cols[...])
    left = jnp.concatenate([vec_rows[...], prod[:, cols:]], 0)
    right = jnp.concatenate([upd_cols, vec_cols[...]], 0)
    out[...] = matrix[...] - mm3(left, right, TN)


def call(kernel, shapes, *args, scratch=(), cost=None, vmem=VMEM_BYTES):
    outs = [jax.ShapeDtypeStruct(s, jnp.float32) for s in shapes]
    return pl.pallas_call(
        kernel,
        out_shape=outs,
        scratch_shapes=[pltpu.VMEM(s, jnp.float32) for s in scratch],
        compiler_params=pltpu.CompilerParams(vmem_limit_bytes=vmem),
        cost_estimate=cost,
    )(*args)


def exchange(blocks, axis):
    return lax.all_to_all(blocks, axis, 0, 0)


def local(matrix, panel):
    rows, cols = matrix.shape
    n_row, n_col = lax.axis_size("prow"), lax.axis_size("pcol")
    block_t = jnp.broadcast_to(panel.T[None], (n_col, SUB, rows))
    rows_t = exchange(block_t, "pcol").reshape(NB, rows)
    (sent,) = call(gram_kernel, [(n_row, HALF, 2 * NB + rows)], rows_t)
    small, blocks = call(
        sort_kernel, [(n_col, HALF, 5 * NB), (HALF, cols)], exchange(sent, "prow")
    )
    band, inv_s, lower, tfac = call(
        factor_kernel,
        [(NB, NB)] * 4,
        exchange(small, "pcol"),
        scratch=[(NB, NB)] * 5,
        cost=pl.CostEstimate(flops=2 * 10**10, bytes_accessed=2**20, transcendentals=0),
        vmem=8 * 2**20,
    )
    vec_rows, sent = call(
        product_kernel,
        [(NB, rows), (n_row, SUB, cols)],
        rows_t,
        blocks,
        matrix,
        inv_s,
        lower,
    )
    vec_cols, sent = call(
        reduce_kernel,
        [(NB, cols), (n_col, HALF, cols + NB)],
        exchange(sent, "prow"),
        inv_s,
        lower,
        scratch=[(NB, cols)],
    )
    wide = lane_ceil(cols + rows) + NB
    (sent,) = call(spread_kernel, [(n_row, HALF, wide)], exchange(sent, "pcol"))
    (trailing,) = call(
        update_kernel,
        [(rows, cols)],
        vec_rows,
        vec_cols,
        exchange(sent, "prow"),
        matrix,
        tfac,
        scratch=[(NB, wide)],
    )
    return (trailing, band)


def solution(mesh):
    specs = (P("prow", "pcol"), P("prow", "pcol"))
    return jax.shard_map(
        local, mesh=mesh, in_specs=specs, out_specs=(P("prow", "pcol"), P()), check_vma=False
    )
```

```python
import jax
import jax.numpy as jnp
from jax import lax
from jax.experimental import pallas as pl
from jax.experimental.pallas import tpu as pltpu
from jax.sharding import PartitionSpec as P

PRECISE = lax.Precision.HIGHEST
VMEM_BYTES = 24 * 2**20
NB = 128
SUB = 8
HALF = SUB // 2
STEP = 4


def mm(left, right, contract=((1,), (0,))):
    return lax.dot_general(
        left, right, (contract, ((), ())), precision=PRECISE, preferred_element_type=jnp.float32
    )


def lane_ceil(count):
    return -(-count // NB) * NB


def halves(block):
    high = block.astype(jnp.bfloat16)
    return high, (block - high.astype(jnp.float32)).astype(jnp.bfloat16)


def mm3(left, right, contract=((1,), (0,))):
    left_high, left_low = halves(left)
    right_high, right_low = halves(right)

    def dot(a, b):
        return lax.dot_general(a, b, (contract, ((), ())), preferred_element_type=jnp.float32)

    return dot(left_high, right_high) + (dot(left_high, right_low) + dot(left_low, right_high))


NT = ((1,), (1,))
TN = ((0,), (0,))


def first_rows_zeroed(block, is_first):
    lanes = lax.broadcasted_iota(jnp.int32, block.shape, 1)
    return jnp.where(is_first & (lanes < NB), 0.0, block)


def gram_kernel(rows_t, sent):
    j = lax.axis_index("pcol")
    own = pl.ds(pl.multiple_of(j * SUB, SUB), SUB)
    block = rows_t[own, :]
    gram = mm(block, rows_t[...], NT)
    first = rows_t[:SUB, :NB]
    extra = jnp.where(j == 1, first[:HALF], first[HALF:])
    pad = jnp.zeros((HALF, rows_t.shape[1] - 3 * NB), jnp.float32)
    top = jnp.concatenate([block[:HALF, :NB], block[HALF:, :NB], extra, pad], 1)
    use_top = (lax.axis_index("prow") == 0) & (j > 0)
    for dest in range(sent.shape[0]):
        sent[dest, :, :NB] = gram[:HALF]
        sent[dest, :, NB : 2 * NB] = gram[HALF:]
        piece = rows_t[dest * HALF : (dest + 1) * HALF, :]
        sent[dest, :, 2 * NB :] = jnp.where(use_top, top, piece)


def sort_kernel(got, small, blocks):
    j = lax.axis_index("pcol")
    gram = jnp.sum(got[:, :, : 2 * NB], axis=0)
    top = got[0, :, 2 * NB : 5 * NB]
    left = got[2 * j, :, 2 * NB :]
    right = got[2 * j + 1, :, 2 * NB :]
    both = jnp.concatenate([left, right], 1)
    for dest in range(small.shape[0]):
        small[dest, :, : 2 * NB] = gram
        small[dest, :, 2 * NB :] = top
    blocks[...] = both


def vectors(panel_t, combine, low, is_first, product=mm):
    vec = product(combine, first_rows_zeroed(panel_t, is_first), TN)
    head = vec[:, :NB] + low.T * jnp.where(is_first, 1.0, 0.0)
    return jnp.concatenate([head, vec[:, NB:]], 1)


def product_kernel(rows_t, blocks, matrix, inv_s, lower, vec_rows, sent):
    vec = vectors(rows_t[...], -inv_s[...], lower[...], lax.axis_index("prow") == 0)
    vec_rows[...] = vec
    part = mm(vec, matrix[...])
    block = blocks[...]
    for dest in range(sent.shape[0]):
        sent[dest, :HALF, :] = part[dest * HALF : (dest + 1) * HALF]
        sent[dest, HALF:, :] = block


def reduce_kernel(got, inv_s, lower, vec_cols, sent, cols_t):
    cols = vec_cols.shape[1]
    for part in range(got.shape[0]):
        cols_t[part * HALF : (part + 1) * HALF, :] = got[part, HALF:, :]
    vec = vectors(cols_t[...], -inv_s[...], lower[...], lax.axis_index("pcol") == 0, mm3)
    vec_cols[...] = vec
    total = jnp.sum(got[...], axis=0)[:HALF]
    small = mm3(total, vec, NT)
    for dest in range(sent.shape[0]):
        sent[dest, :, :cols] = total
        sent[dest, :, cols:] = small


def spread_kernel(got, sent):
    cols = got.shape[2] - NB
    rows = cols // 2
    at = lane_ceil(cols + rows)
    own = got[lax.axis_index("pcol"), :, :cols]
    small = jnp.sum(got[:, :, cols:], axis=0)
    for part in range(got.shape[0]):
        whole = got[part, :, :cols]
        for half in range(2):
            dest = 2 * part + half
            sent[dest, :, :cols] = own
            sent[dest, :, cols : cols + rows] = whole[:, half * rows : (half + 1) * rows]
            sent[dest, :, cols + rows : at] = jnp.zeros((HALF, at - cols - rows), jnp.float32)
            sent[dest, :, at:] = small


def factor_kernel(got, band, inv_s, lower, tfac, work, inv_c, rest, inv_l, upper):
    rows = lax.broadcasted_iota(jnp.int32, (NB, NB), 0)
    lanes = lax.broadcasted_iota(jnp.int32, (NB, NB), 1)
    lane = lax.broadcasted_iota(jnp.int32, (1, NB), 1)
    eye = jnp.where(rows == lanes, 1.0, 0.0)
    for part in range(got.shape[0]):
        for half in range(2):
            to = slice(part * SUB + half * HALF, part * SUB + (half + 1) * HALF)
            work[to, :] = got[part, :, half * NB : (half + 1) * NB]
            source, at = (half + 1, 4) if part == 0 else (part, 2 + half)
            rest[to, :] = -got[source, :, at * NB : (at + 1) * NB]
    rest[...] = rest[...].T
    for ref in (inv_c, inv_l, inv_s, lower):
        ref[...] = eye

    def spread(column):
        return jnp.broadcast_to(column, (column.shape[0], NB))

    for first in range(0, NB, STEP):
        lo = first // SUB * SUB
        hi = lo + SUB
        block = range(first, first + STEP)
        row_at = rows[lo:]
        gram_col = [spread(work[lo:, k : k + 1]) for k in block]
        rest_col = [spread(rest[lo:, k : k + 1]) for k in block]
        inv_col = [spread(inv_s[:hi, k : k + 1]) for k in block]
        gram_row = [work[k : k + 1, :] for k in block]
        rest_row = [rest[k : k + 1, :] for k in block]
        c_inv_row = [inv_c[k : k + 1, :] for k in block]
        l_inv_row = [inv_l[k : k + 1, :] for k in block]
        done = []
        for t, k in enumerate(block):
            here = slice(k - lo, k - lo + 1)
            pivot = gram_col[t][here]
            inv = lax.rsqrt(pivot)
            c_col = jnp.where(row_at > k, gram_col[t] * inv, 0.0)
            c_row = jnp.where(lane >= k, gram_row[t] * inv, 0.0)
            x_row = c_inv_row[t] * inv
            s_row = jnp.where(lane >= k, rest_row[t] - c_row, 0.0)
            scale = 1.0 / (rest_col[t][here] - pivot * inv)
            l_col = jnp.where(row_at > k, rest_col[t] * scale, 0.0)
            right = jnp.where(lane > k, s_row, 0.0)
            x_col = inv_col[t] * scale
            l_row = l_inv_row[t]
            band[k : k + 1, :] = -c_row
            upper[k : k + 1, :] = s_row
            for u in range(t + 1, STEP):
                there = slice(first + u - lo, first + u - lo + 1)
                c, l = c_col[there], l_col[there]
                s = rest_col[u][here] - c
                gram_col[u] = gram_col[u] - c_col * c
                rest_col[u] = rest_col[u] - l_col * s
                inv_col[u] = inv_col[u] - x_col * s
                gram_row[u] = gram_row[u] - c * c_row
                c_inv_row[u] = c_inv_row[u] - c * x_row
                rest_row[u] = rest_row[u] - l * right
                l_inv_row[u] = l_inv_row[u] - l * l_row
            done.append((c_col, c_row, x_row, l_col, l_row, right, x_col))
        below = (first + STEP) // SUB * SUB
        if below < NB:
            for ref, col, row in ((work, 0, 1), (rest, 3, 5), (inv_c, 0, 2), (inv_l, 3, 4)):
                total = ref[below:, :]
                for terms in done:
                    total = total - terms[col][below - lo :] * terms[row]
                ref[below:, :] = total
        above = inv_s[:hi, :]
        for terms in done:
            above = above - terms[6] * terms[5]
        low = lower[lo:, :]
        for k, terms in zip(block, done):
            above = jnp.where(lanes[:hi] == k, terms[6], above)
            low = jnp.where((lanes[lo:] == k) & (row_at > k), terms[3], low)
            inv_c[k : k + 1, :] = terms[2]
            inv_l[k : k + 1, :] = terms[4]
        inv_s[:hi, :] = above
        lower[lo:, :] = low
    tfac[...] = -mm(upper[...], mm(inv_l[...], inv_c[...]), NT)


def update_kernel(vec_rows, vec_cols, got, matrix, tfac, out, moved, block, left_done):
    rows, cols = matrix.shape
    at = lane_ceil(cols + rows)
    for part in range(got.shape[0]):
        moved[part * HALF : (part + 1) * HALF, :] = got[part]
    t = tfac[...]
    mid = mm3(t, mm3(moved[:, at:], t), TN)
    prod = mm3(t, moved[:, : cols + rows], TN)
    upd_cols = prod[:, :cols] - mm3(0.5 * (mid + mid.T), vec_cols[...])
    left = jnp.concatenate([vec_rows[...], prod[:, cols:]], 0)
    right = jnp.concatenate([upd_cols, vec_cols[...]], 0)
    sends = []
    for at, stripe in enumerate((slice(0, 3 * NB), slice(3 * NB, 5 * NB), slice(5 * NB, cols))):
        block[:, stripe] = matrix[:, stripe] - mm3(left, right[:, stripe], TN)
        send = pltpu.make_async_copy(block.at[:, stripe], out.at[:, stripe], left_done.at[at])
        send.start()
        sends.append(send)
    for send in sends:
        send.wait()


def call(kernel, shapes, *args, scratch=(), cost=None, vmem=VMEM_BYTES):
    outs = [jax.ShapeDtypeStruct(s, jnp.float32) for s in shapes]
    return pl.pallas_call(
        kernel,
        out_shape=outs,
        scratch_shapes=[pltpu.VMEM(s, jnp.float32) for s in scratch],
        compiler_params=pltpu.CompilerParams(vmem_limit_bytes=vmem),
        cost_estimate=cost,
    )(*args)


def exchange(blocks, axis):
    return lax.all_to_all(blocks, axis, 0, 0)


def local(matrix, panel):
    rows, cols = matrix.shape
    n_row, n_col = lax.axis_size("prow"), lax.axis_size("pcol")
    block_t = jnp.broadcast_to(panel.T[None], (n_col, SUB, rows))
    rows_t = exchange(block_t, "pcol").reshape(NB, rows)
    (sent,) = call(gram_kernel, [(n_row, HALF, 2 * NB + rows)], rows_t)
    small, blocks = call(
        sort_kernel, [(n_col, HALF, 5 * NB), (HALF, cols)], exchange(sent, "prow")
    )
    band, inv_s, lower, tfac = call(
        factor_kernel,
        [(NB, NB)] * 4,
        exchange(small, "pcol"),
        scratch=[(NB, NB)] * 5,
        cost=pl.CostEstimate(flops=2 * 10**10, bytes_accessed=2**20, transcendentals=0),
        vmem=8 * 2**20,
    )
    vec_rows, sent = call(
        product_kernel,
        [(NB, rows), (n_row, SUB, cols)],
        rows_t,
        blocks,
        matrix,
        inv_s,
        lower,
    )
    vec_cols, sent = call(
        reduce_kernel,
        [(NB, cols), (n_col, HALF, cols + NB)],
        exchange(sent, "prow"),
        inv_s,
        lower,
        scratch=[(NB, cols)],
    )
    wide = lane_ceil(cols + rows) + NB
    (sent,) = call(spread_kernel, [(n_row, HALF, wide)], exchange(sent, "pcol"))
    vmem, hbm = pl.BlockSpec(memory_space=pltpu.VMEM), pl.BlockSpec(memory_space=pl.ANY)
    trailing = pl.pallas_call(
        update_kernel,
        out_shape=jax.ShapeDtypeStruct((rows, cols), jnp.float32),
        in_specs=[vmem] * 5,
        out_specs=hbm,
        scratch_shapes=[
            pltpu.VMEM((NB, wide), jnp.float32),
            pltpu.VMEM((rows, cols), jnp.float32),
            pltpu.SemaphoreType.DMA((3,)),
        ],
        compiler_params=pltpu.CompilerParams(vmem_limit_bytes=VMEM_BYTES),
    )(vec_rows, vec_cols, exchange(sent, "prow"), matrix, tfac)
    return (trailing, band)


def solution(mesh):
    specs = (P("prow", "pcol"), P("prow", "pcol"))
    return jax.shard_map(
        local, mesh=mesh, in_specs=specs, out_specs=(P("prow", "pcol"), P()), check_vma=False
    )
```

```python
import jax
import jax.numpy as jnp
from jax import lax
from jax.experimental import pallas as pl
from jax.experimental.pallas import tpu as pltpu
from jax.sharding import PartitionSpec as P

PRECISE = lax.Precision.HIGHEST
VMEM_BYTES = 24 * 2**20
NB = 128
SUB = 8
HALF = SUB // 2
STEP = 4


def mm(left, right, contract=((1,), (0,))):
    return lax.dot_general(
        left, right, (contract, ((), ())), precision=PRECISE, preferred_element_type=jnp.float32
    )


def lane_ceil(count):
    return -(-count // NB) * NB


def halves(block):
    high = block.astype(jnp.bfloat16)
    return high, (block - high.astype(jnp.float32)).astype(jnp.bfloat16)


def mm3(left, right, contract=((1,), (0,))):
    left_high, left_low = halves(left)
    right_high, right_low = halves(right)

    def dot(a, b):
        return lax.dot_general(a, b, (contract, ((), ())), preferred_element_type=jnp.float32)

    return dot(left_high, right_high) + (dot(left_high, right_low) + dot(left_low, right_high))


NT = ((1,), (1,))
TN = ((0,), (0,))


def first_rows_zeroed(block, is_first):
    lanes = lax.broadcasted_iota(jnp.int32, block.shape, 1)
    return jnp.where(is_first & (lanes < NB), 0.0, block)


def gram_kernel(rows_t, sent):
    j = lax.axis_index("pcol")
    own = pl.ds(pl.multiple_of(j * SUB, SUB), SUB)
    block = rows_t[own, :]
    gram = mm(block, rows_t[...], NT)
    first = rows_t[:SUB, :NB]
    extra = jnp.where(j == 1, first[:HALF], first[HALF:])
    pad = jnp.zeros((HALF, rows_t.shape[1] - 3 * NB), jnp.float32)
    top = jnp.concatenate([block[:HALF, :NB], block[HALF:, :NB], extra, pad], 1)
    use_top = (lax.axis_index("prow") == 0) & (j > 0)
    for dest in range(sent.shape[0]):
        sent[dest, :, :NB] = gram[:HALF]
        sent[dest, :, NB : 2 * NB] = gram[HALF:]
        piece = rows_t[dest * HALF : (dest + 1) * HALF, :]
        sent[dest, :, 2 * NB :] = jnp.where(use_top, top, piece)


def sort_kernel(got, small, blocks):
    j = lax.axis_index("pcol")
    gram = jnp.sum(got[:, :, : 2 * NB], axis=0)
    top = got[0, :, 2 * NB : 5 * NB]
    left = got[2 * j, :, 2 * NB :]
    right = got[2 * j + 1, :, 2 * NB :]
    both = jnp.concatenate([left, right], 1)
    for dest in range(small.shape[0]):
        small[dest, :, : 2 * NB] = gram
        small[dest, :, 2 * NB :] = top
    blocks[...] = both


def vectors(panel_t, combine, low, is_first, product=mm):
    vec = product(combine, first_rows_zeroed(panel_t, is_first), TN)
    head = vec[:, :NB] + low.T * jnp.where(is_first, 1.0, 0.0)
    return jnp.concatenate([head, vec[:, NB:]], 1)


def product_kernel(rows_t, blocks, matrix, inv_s, lower, vec_rows, sent):
    vec = vectors(rows_t[...], -inv_s[...], lower[...], lax.axis_index("prow") == 0)
    vec_rows[...] = vec
    part = mm3(vec, matrix[...])
    block = blocks[...]
    for dest in range(sent.shape[0]):
        sent[dest, :HALF, :] = part[dest * HALF : (dest + 1) * HALF]
        sent[dest, HALF:, :] = block


def reduce_kernel(got, inv_s, lower, vec_cols, sent, cols_t):
    cols = vec_cols.shape[1]
    for part in range(got.shape[0]):
        cols_t[part * HALF : (part + 1) * HALF, :] = got[part, HALF:, :]
    vec = vectors(cols_t[...], -inv_s[...], lower[...], lax.axis_index("pcol") == 0, mm3)
    vec_cols[...] = vec
    total = jnp.sum(got[...], axis=0)[:HALF]
    small = mm3(total, vec, NT)
    for dest in range(sent.shape[0]):
        sent[dest, :, :cols] = total
        sent[dest, :, cols:] = small


def spread_kernel(got, sent):
    cols = got.shape[2] - NB
    rows = cols // 2
    at = lane_ceil(cols + rows)
    own = got[lax.axis_index("pcol"), :, :cols]
    small = jnp.sum(got[:, :, cols:], axis=0)
    for part in range(got.shape[0]):
        whole = got[part, :, :cols]
        for half in range(2):
            dest = 2 * part + half
            sent[dest, :, :cols] = own
            sent[dest, :, cols : cols + rows] = whole[:, half * rows : (half + 1) * rows]
            sent[dest, :, cols + rows : at] = jnp.zeros((HALF, at - cols - rows), jnp.float32)
            sent[dest, :, at:] = small


def factor_kernel(got, band, inv_s, lower, tfac, work, inv_c, rest, inv_l, upper):
    rows = lax.broadcasted_iota(jnp.int32, (NB, NB), 0)
    lanes = lax.broadcasted_iota(jnp.int32, (NB, NB), 1)
    lane = lax.broadcasted_iota(jnp.int32, (1, NB), 1)
    eye = jnp.where(rows == lanes, 1.0, 0.0)
    for part in range(got.shape[0]):
        for half in range(2):
            to = slice(part * SUB + half * HALF, part * SUB + (half + 1) * HALF)
            work[to, :] = got[part, :, half * NB : (half + 1) * NB]
            source, at = (half + 1, 4) if part == 0 else (part, 2 + half)
            rest[to, :] = -got[source, :, at * NB : (at + 1) * NB]
    rest[...] = rest[...].T
    for ref in (inv_c, inv_l, inv_s, lower):
        ref[...] = eye

    def spread(column):
        return jnp.broadcast_to(column, (column.shape[0], NB))

    for first in range(0, NB, STEP):
        lo = first // SUB * SUB
        hi = lo + SUB
        block = range(first, first + STEP)
        row_at = rows[lo:]
        gram_col = [spread(work[lo:, k : k + 1]) for k in block]
        rest_col = [spread(rest[lo:, k : k + 1]) for k in block]
        inv_col = [spread(inv_s[:hi, k : k + 1]) for k in block]
        gram_row = [work[k : k + 1, :] for k in block]
        rest_row = [rest[k : k + 1, :] for k in block]
        c_inv_row = [inv_c[k : k + 1, :] for k in block]
        l_inv_row = [inv_l[k : k + 1, :] for k in block]
        done = []
        for t, k in enumerate(block):
            here = slice(k - lo, k - lo + 1)
            pivot = gram_col[t][here]
            inv = lax.rsqrt(pivot)
            c_col = jnp.where(row_at > k, gram_col[t] * inv, 0.0)
            c_row = jnp.where(lane >= k, gram_row[t] * inv, 0.0)
            x_row = c_inv_row[t] * inv
            s_row = jnp.where(lane >= k, rest_row[t] - c_row, 0.0)
            scale = 1.0 / (rest_col[t][here] - pivot * inv)
            l_col = jnp.where(row_at > k, rest_col[t] * scale, 0.0)
            right = jnp.where(lane > k, s_row, 0.0)
            x_col = inv_col[t] * scale
            l_row = l_inv_row[t]
            band[k : k + 1, :] = -c_row
            upper[k : k + 1, :] = s_row
            for u in range(t + 1, STEP):
                there = slice(first + u - lo, first + u - lo + 1)
                c, l = c_col[there], l_col[there]
                s = rest_col[u][here] - c
                gram_col[u] = gram_col[u] - c_col * c
                rest_col[u] = rest_col[u] - l_col * s
                inv_col[u] = inv_col[u] - x_col * s
                gram_row[u] = gram_row[u] - c * c_row
                c_inv_row[u] = c_inv_row[u] - c * x_row
                rest_row[u] = rest_row[u] - l * right
                l_inv_row[u] = l_inv_row[u] - l * l_row
            done.append((c_col, c_row, x_row, l_col, l_row, right, x_col))
        below = (first + STEP) // SUB * SUB
        if below < NB:
            for ref, col, row in ((work, 0, 1), (rest, 3, 5), (inv_c, 0, 2), (inv_l, 3, 4)):
                total = ref[below:, :]
                for terms in done:
                    total = total - terms[col][below - lo :] * terms[row]
                ref[below:, :] = total
        above = inv_s[:hi, :]
        for terms in done:
            above = above - terms[6] * terms[5]
        low = lower[lo:, :]
        for k, terms in zip(block, done):
            above = jnp.where(lanes[:hi] == k, terms[6], above)
            low = jnp.where((lanes[lo:] == k) & (row_at > k), terms[3], low)
            inv_c[k : k + 1, :] = terms[2]
            inv_l[k : k + 1, :] = terms[4]
        inv_s[:hi, :] = above
        lower[lo:, :] = low
    tfac[...] = -mm(upper[...], mm(inv_l[...], inv_c[...]), NT)


def update_kernel(vec_rows, vec_cols, got, matrix, tfac, out, moved, block, left_done):
    rows, cols = matrix.shape
    at = lane_ceil(cols + rows)
    for part in range(got.shape[0]):
        moved[part * HALF : (part + 1) * HALF, :] = got[part]
    t = tfac[...]
    mid = mm3(t, mm3(moved[:, at:], t), TN)
    prod = mm3(t, moved[:, : cols + rows], TN)
    upd_cols = prod[:, :cols] - mm3(0.5 * (mid + mid.T), vec_cols[...])
    left = jnp.concatenate([vec_rows[...], prod[:, cols:]], 0)
    right = jnp.concatenate([upd_cols, vec_cols[...]], 0)
    sends = []
    for at, stripe in enumerate((slice(0, 3 * NB), slice(3 * NB, 5 * NB), slice(5 * NB, cols))):
        block[:, stripe] = matrix[:, stripe] - mm3(left, right[:, stripe], TN)
        send = pltpu.make_async_copy(block.at[:, stripe], out.at[:, stripe], left_done.at[at])
        send.start()
        sends.append(send)
    for send in sends:
        send.wait()


def call(kernel, shapes, *args, scratch=(), cost=None, vmem=VMEM_BYTES):
    outs = [jax.ShapeDtypeStruct(s, jnp.float32) for s in shapes]
    return pl.pallas_call(
        kernel,
        out_shape=outs,
        scratch_shapes=[pltpu.VMEM(s, jnp.float32) for s in scratch],
        compiler_params=pltpu.CompilerParams(vmem_limit_bytes=vmem),
        cost_estimate=cost,
    )(*args)


def exchange(blocks, axis):
    return lax.all_to_all(blocks, axis, 0, 0)


def local(matrix, panel):
    rows, cols = matrix.shape
    n_row, n_col = lax.axis_size("prow"), lax.axis_size("pcol")
    block_t = jnp.broadcast_to(panel.T[None], (n_col, SUB, rows))
    rows_t = exchange(block_t, "pcol").reshape(NB, rows)
    (sent,) = call(gram_kernel, [(n_row, HALF, 2 * NB + rows)], rows_t)
    small, blocks = call(
        sort_kernel, [(n_col, HALF, 5 * NB), (HALF, cols)], exchange(sent, "prow")
    )
    band, inv_s, lower, tfac = call(
        factor_kernel,
        [(NB, NB)] * 4,
        exchange(small, "pcol"),
        scratch=[(NB, NB)] * 5,
        cost=pl.CostEstimate(flops=2 * 10**10, bytes_accessed=2**20, transcendentals=0),
        vmem=8 * 2**20,
    )
    vec_rows, sent = call(
        product_kernel,
        [(NB, rows), (n_row, SUB, cols)],
        rows_t,
        blocks,
        matrix,
        inv_s,
        lower,
    )
    vec_cols, sent = call(
        reduce_kernel,
        [(NB, cols), (n_col, HALF, cols + NB)],
        exchange(sent, "prow"),
        inv_s,
        lower,
        scratch=[(NB, cols)],
    )
    wide = lane_ceil(cols + rows) + NB
    (sent,) = call(spread_kernel, [(n_row, HALF, wide)], exchange(sent, "pcol"))
    vmem, hbm = pl.BlockSpec(memory_space=pltpu.VMEM), pl.BlockSpec(memory_space=pl.ANY)
    trailing = pl.pallas_call(
        update_kernel,
        out_shape=jax.ShapeDtypeStruct((rows, cols), jnp.float32),
        in_specs=[vmem] * 5,
        out_specs=hbm,
        scratch_shapes=[
            pltpu.VMEM((NB, wide), jnp.float32),
            pltpu.VMEM((rows, cols), jnp.float32),
            pltpu.SemaphoreType.DMA((3,)),
        ],
        compiler_params=pltpu.CompilerParams(vmem_limit_bytes=VMEM_BYTES),
    )(vec_rows, vec_cols, exchange(sent, "prow"), matrix, tfac)
    return (trailing, band)


def solution(mesh):
    specs = (P("prow", "pcol"), P("prow", "pcol"))
    return jax.shard_map(
        local, mesh=mesh, in_specs=specs, out_specs=(P("prow", "pcol"), P()), check_vma=False
    )
```

```python
import jax
import jax.numpy as jnp
from jax import lax
from jax.experimental import pallas as pl
from jax.experimental.pallas import tpu as pltpu
from jax.sharding import PartitionSpec as P

PRECISE = lax.Precision.HIGHEST
VMEM_BYTES = 24 * 2**20
NB = 128
SUB = 8
HALF = SUB // 2
STEP = 4


def mm(left, right, contract=((1,), (0,))):
    return lax.dot_general(
        left, right, (contract, ((), ())), precision=PRECISE, preferred_element_type=jnp.float32
    )


def lane_ceil(count):
    return -(-count // NB) * NB


def halves(block):
    high = block.astype(jnp.bfloat16)
    return high, (block - high.astype(jnp.float32)).astype(jnp.bfloat16)


def mm3(left, right, contract=((1,), (0,))):
    left_high, left_low = halves(left)
    right_high, right_low = halves(right)

    def dot(a, b):
        return lax.dot_general(a, b, (contract, ((), ())), preferred_element_type=jnp.float32)

    return dot(left_high, right_high) + (dot(left_high, right_low) + dot(left_low, right_high))


NT = ((1,), (1,))
TN = ((0,), (0,))


def first_rows_zeroed(block, is_first):
    lanes = lax.broadcasted_iota(jnp.int32, block.shape, 1)
    return jnp.where(is_first & (lanes < NB), 0.0, block)


def gram_kernel(rows_t, sent):
    j = lax.axis_index("pcol")
    own = pl.ds(pl.multiple_of(j * SUB, SUB), SUB)
    block = rows_t[own, :]
    gram = mm(block, rows_t[...], NT)
    first = rows_t[:SUB, :NB]
    extra = jnp.where(j == 1, first[:HALF], first[HALF:])
    pad = jnp.zeros((HALF, rows_t.shape[1] - 3 * NB), jnp.float32)
    top = jnp.concatenate([block[:HALF, :NB], block[HALF:, :NB], extra, pad], 1)
    use_top = (lax.axis_index("prow") == 0) & (j > 0)
    for dest in range(sent.shape[0]):
        sent[dest, :, :NB] = gram[:HALF]
        sent[dest, :, NB : 2 * NB] = gram[HALF:]
        piece = rows_t[dest * HALF : (dest + 1) * HALF, :]
        sent[dest, :, 2 * NB :] = jnp.where(use_top, top, piece)


def sort_kernel(got, small, blocks):
    j = lax.axis_index("pcol")
    gram = jnp.sum(got[:, :, : 2 * NB], axis=0)
    top = got[0, :, 2 * NB : 5 * NB]
    left = got[2 * j, :, 2 * NB :]
    right = got[2 * j + 1, :, 2 * NB :]
    both = jnp.concatenate([left, right], 1)
    for dest in range(small.shape[0]):
        small[dest, :, : 2 * NB] = gram
        small[dest, :, 2 * NB :] = top
    blocks[...] = both


def vectors(panel_t, combine, low, is_first):
    vec = mm(combine, first_rows_zeroed(panel_t, is_first), TN)
    head = vec[:, :NB] + low.T * jnp.where(is_first, 1.0, 0.0)
    return jnp.concatenate([head, vec[:, NB:]], 1)


def product_kernel(rows_t, blocks, matrix, inv_s, lower, vec_rows, sent):
    vec = vectors(rows_t[...], -inv_s[...], lower[...], lax.axis_index("prow") == 0)
    vec_rows[...] = vec
    part = mm3(vec, matrix[...])
    block = blocks[...]
    for dest in range(sent.shape[0]):
        sent[dest, :HALF, :] = part[dest * HALF : (dest + 1) * HALF]
        sent[dest, HALF:, :] = block


def reduce_kernel(got, inv_s, lower, vec_cols, sent, cols_t):
    cols = vec_cols.shape[1]
    for part in range(got.shape[0]):
        cols_t[part * HALF : (part + 1) * HALF, :] = got[part, HALF:, :]
    vec = vectors(cols_t[...], -inv_s[...], lower[...], lax.axis_index("pcol") == 0)
    vec_cols[...] = vec
    total = jnp.sum(got[...], axis=0)[:HALF]
    small = mm3(total, vec, NT)
    for dest in range(sent.shape[0]):
        sent[dest, :, :cols] = total
        sent[dest, :, cols:] = small


def spread_kernel(got, sent):
    cols = got.shape[2] - NB
    rows = cols // 2
    at = lane_ceil(cols + rows)
    own = got[lax.axis_index("pcol"), :, :cols]
    small = jnp.sum(got[:, :, cols:], axis=0)
    for part in range(got.shape[0]):
        whole = got[part, :, :cols]
        for half in range(2):
            dest = 2 * part + half
            sent[dest, :, :cols] = own
            sent[dest, :, cols : cols + rows] = whole[:, half * rows : (half + 1) * rows]
            sent[dest, :, cols + rows : at] = jnp.zeros((HALF, at - cols - rows), jnp.float32)
            sent[dest, :, at:] = small


def factor_kernel(got, band, inv_s, lower, tfac, work, inv_c, rest, inv_l, upper):
    rows = lax.broadcasted_iota(jnp.int32, (NB, NB), 0)
    lanes = lax.broadcasted_iota(jnp.int32, (NB, NB), 1)
    lane = lax.broadcasted_iota(jnp.int32, (1, NB), 1)
    eye = jnp.where(rows == lanes, 1.0, 0.0)
    for part in range(got.shape[0]):
        for half in range(2):
            to = slice(part * SUB + half * HALF, part * SUB + (half + 1) * HALF)
            work[to, :] = got[part, :, half * NB : (half + 1) * NB]
            source, at = (half + 1, 4) if part == 0 else (part, 2 + half)
            rest[to, :] = -got[source, :, at * NB : (at + 1) * NB]
    rest[...] = rest[...].T
    for ref in (inv_c, inv_l, inv_s, lower):
        ref[...] = eye

    def spread(column):
        return jnp.broadcast_to(column, (column.shape[0], NB))

    for first in range(0, NB, STEP):
        lo = first // SUB * SUB
        hi = lo + SUB
        block = range(first, first + STEP)
        row_at = rows[lo:]
        gram_col = [spread(work[lo:, k : k + 1]) for k in block]
        rest_col = [spread(rest[lo:, k : k + 1]) for k in block]
        inv_col = [spread(inv_s[:hi, k : k + 1]) for k in block]
        gram_row = [work[k : k + 1, :] for k in block]
        rest_row = [rest[k : k + 1, :] for k in block]
        c_inv_row = [inv_c[k : k + 1, :] for k in block]
        l_inv_row = [inv_l[k : k + 1, :] for k in block]
        done = []
        for t, k in enumerate(block):
            here = slice(k - lo, k - lo + 1)
            pivot = gram_col[t][here]
            inv = lax.rsqrt(pivot)
            c_col = jnp.where(row_at > k, gram_col[t] * inv, 0.0)
            c_row = jnp.where(lane >= k, gram_row[t] * inv, 0.0)
            x_row = c_inv_row[t] * inv
            s_row = jnp.where(lane >= k, rest_row[t] - c_row, 0.0)
            scale = 1.0 / (rest_col[t][here] - pivot * inv)
            l_col = jnp.where(row_at > k, rest_col[t] * scale, 0.0)
            right = jnp.where(lane > k, s_row, 0.0)
            x_col = inv_col[t] * scale
            l_row = l_inv_row[t]
            band[k : k + 1, :] = -c_row
            upper[k : k + 1, :] = s_row
            for u in range(t + 1, STEP):
                there = slice(first + u - lo, first + u - lo + 1)
                c, l = c_col[there], l_col[there]
                s = rest_col[u][here] - c
                gram_col[u] = gram_col[u] - c_col * c
                rest_col[u] = rest_col[u] - l_col * s
                inv_col[u] = inv_col[u] - x_col * s
                gram_row[u] = gram_row[u] - c * c_row
                c_inv_row[u] = c_inv_row[u] - c * x_row
                rest_row[u] = rest_row[u] - l * right
                l_inv_row[u] = l_inv_row[u] - l * l_row
            done.append((c_col, c_row, x_row, l_col, l_row, right, x_col))
        below = (first + STEP) // SUB * SUB
        if below < NB:
            for ref, col, row in ((work, 0, 1), (rest, 3, 5), (inv_c, 0, 2), (inv_l, 3, 4)):
                total = ref[below:, :]
                for terms in done:
                    total = total - terms[col][below - lo :] * terms[row]
                ref[below:, :] = total
        above = inv_s[:hi, :]
        for terms in done:
            above = above - terms[6] * terms[5]
        low = lower[lo:, :]
        for k, terms in zip(block, done):
            above = jnp.where(lanes[:hi] == k, terms[6], above)
            low = jnp.where((lanes[lo:] == k) & (row_at > k), terms[3], low)
            inv_c[k : k + 1, :] = terms[2]
            inv_l[k : k + 1, :] = terms[4]
        inv_s[:hi, :] = above
        lower[lo:, :] = low
    tfac[...] = -mm(upper[...], mm(inv_l[...], inv_c[...]), NT)


def update_kernel(vec_rows, vec_cols, got, matrix, tfac, out, moved, block, left_done):
    rows, cols = matrix.shape
    at = lane_ceil(cols + rows)
    for part in range(got.shape[0]):
        moved[part * HALF : (part + 1) * HALF, :] = got[part]
    t = tfac[...]
    mid = mm3(t, mm3(moved[:, at:], t), TN)
    prod = mm3(t, moved[:, : cols + rows], TN)
    upd_cols = prod[:, :cols] - mm3(0.5 * (mid + mid.T), vec_cols[...])
    left = jnp.concatenate([vec_rows[...], prod[:, cols:]], 0)
    right = jnp.concatenate([upd_cols, vec_cols[...]], 0)
    sends = []
    for at, stripe in enumerate((slice(0, 3 * NB), slice(3 * NB, 5 * NB), slice(5 * NB, cols))):
        block[:, stripe] = matrix[:, stripe] - mm3(left, right[:, stripe], TN)
        send = pltpu.make_async_copy(block.at[:, stripe], out.at[:, stripe], left_done.at[at])
        send.start()
        sends.append(send)
    for send in sends:
        send.wait()


def call(kernel, shapes, *args, scratch=(), cost=None, vmem=VMEM_BYTES):
    outs = [jax.ShapeDtypeStruct(s, jnp.float32) for s in shapes]
    return pl.pallas_call(
        kernel,
        out_shape=outs,
        scratch_shapes=[pltpu.VMEM(s, jnp.float32) for s in scratch],
        compiler_params=pltpu.CompilerParams(vmem_limit_bytes=vmem),
        cost_estimate=cost,
    )(*args)


def exchange(blocks, axis):
    return lax.all_to_all(blocks, axis, 0, 0)


def local(matrix, panel):
    rows, cols = matrix.shape
    n_row, n_col = lax.axis_size("prow"), lax.axis_size("pcol")
    block_t = jnp.broadcast_to(panel.T[None], (n_col, SUB, rows))
    rows_t = exchange(block_t, "pcol").reshape(NB, rows)
    (sent,) = call(gram_kernel, [(n_row, HALF, 2 * NB + rows)], rows_t)
    small, blocks = call(
        sort_kernel, [(n_col, HALF, 5 * NB), (HALF, cols)], exchange(sent, "prow")
    )
    band, inv_s, lower, tfac = call(
        factor_kernel,
        [(NB, NB)] * 4,
        exchange(small, "pcol"),
        scratch=[(NB, NB)] * 5,
        cost=pl.CostEstimate(flops=2 * 10**10, bytes_accessed=2**20, transcendentals=0),
        vmem=8 * 2**20,
    )
    vec_rows, sent = call(
        product_kernel,
        [(NB, rows), (n_row, SUB, cols)],
        rows_t,
        blocks,
        matrix,
        inv_s,
        lower,
    )
    vec_cols, sent = call(
        reduce_kernel,
        [(NB, cols), (n_col, HALF, cols + NB)],
        exchange(sent, "prow"),
        inv_s,
        lower,
        scratch=[(NB, cols)],
    )
    wide = lane_ceil(cols + rows) + NB
    (sent,) = call(spread_kernel, [(n_row, HALF, wide)], exchange(sent, "pcol"))
    vmem, hbm = pl.BlockSpec(memory_space=pltpu.VMEM), pl.BlockSpec(memory_space=pl.ANY)
    trailing = pl.pallas_call(
        update_kernel,
        out_shape=jax.ShapeDtypeStruct((rows, cols), jnp.float32),
        in_specs=[vmem] * 5,
        out_specs=hbm,
        scratch_shapes=[
            pltpu.VMEM((NB, wide), jnp.float32),
            pltpu.VMEM((rows, cols), jnp.float32),
            pltpu.SemaphoreType.DMA((3,)),
        ],
        compiler_params=pltpu.CompilerParams(vmem_limit_bytes=VMEM_BYTES),
    )(vec_rows, vec_cols, exchange(sent, "prow"), matrix, tfac)
    return (trailing, band)


def solution(mesh):
    specs = (P("prow", "pcol"), P("prow", "pcol"))
    return jax.shard_map(
        local, mesh=mesh, in_specs=specs, out_specs=(P("prow", "pcol"), P()), check_vma=False
    )
```
